32 devices in a mesh: groups: 2 (over x), node: 16 (over z, y, core).
Axes of the slice: x: 2, y: 2, z: 4, core: 2. Of those that a mesh axis runs over, the one named last changes fastest.
Arguments:
- query: bfloat16 [256, 6144], P(('groups', 'node')), parts along dimension 0, may hold values from -5 to 5
- new_kv: bfloat16 [256, 2, 1024], P(('groups', 'node')), parts along dimension 0, may hold values from -6 to 6
- cache_kv: bfloat16 [256, 2, 128, 1024], P(('groups', 'node')), parts along dimension 0, may hold values from -200 to 200
- cache_len: int32 [256], P(('groups', 'node')), parts along dimension 0, may hold values from 2 to 128, as said below
- prefix_kv: bfloat16 [512, 2, 1024], P(('groups', 'node')), parts along dimension 0, may hold values from -6 to 6
- residual_in: bfloat16 [256, 6144], P(('groups', 'node')), parts along dimension 0, may hold values from -0.29882812 to 0.29882812
- norm_gain: float32 [6144], replicated, may hold values from 0.25 to 1.75
- router_w: bfloat16 [6144, 16], replicated, may hold values from -0.21875 to 0.21875
- expert_ids: int32 [256, 4], P(('groups', 'node')), parts along dimension 0, may hold values from 0 to 15, as said below
- w_gate: bfloat16 [6144, 10752], P(None, 'node'), may hold values from -0.078125 to 0.078125
- w_up: bfloat16 [6144, 10752], P(None, 'node'), may hold values from -0.078125 to 0.078125
- w_down: bfloat16 [10752, 6144], P('node'), may hold values from -0.125 to 0.125
Outputs:
- layer_out: bfloat16 [256, 6144], P(('groups', 'node')), parts along dimension 0
The draws below stay inside these ranges and needn't reach their ends.
There are 2 independent parts, one for each index of `groups`. The reference program is written for one: setup_inputs(seed, part) draws one part's arguments, and reference() takes and returns one part's arrays. A program takes and returns all parts, laid end to end along the dimension named above; an argument that names none is the same for every part. Nothing has to cross between parts.
Inputs may be any that keep to these rules, and one draw needn't show every extreme that they name: `cache_len`: positions 0 and 1 are always live. `expert_ids`: each row names 4 different experts. Every device's 8 rows hold between 1 and 4 rows that name expert 0.
All inputs are finite; a program needn't handle non-finite values.
Results may differ from the reference program's by a relative error of at most 0.017.
Values may be sent and summed in bfloat16 or wider, within the bound.
A program may use at most 128 MiB of HBM per device.

```python
import jax
import jax.numpy as jnp
from jax import lax

D = 6144
HEADS = 48
KV_HEADS = 8
HEAD = 128
EXPERTS = 16
TOP = 4
FF = 10752
SEQ_DEV = 8
CACHE = 128
CAP = 4
SEQS = 128
PREFIX = 256


def query_base(key):
    return jnp.clip(jax.random.normal(key, (SEQS, HEADS * HEAD), jnp.float32), -5.0, 5.0)


def draw_query(key, part):
    base = query_base(key)
    return base.astype(jnp.bfloat16)


def draw_cache_kv(key, part):
    key = jax.random.fold_in(key, 12)
    k_main = jax.random.fold_in(key, 0)
    cache = jnp.clip(jax.random.normal(k_main, (SEQS, 2, CACHE, KV_HEADS * HEAD), jnp.float32), -6.0, 6.0)
    return cache.astype(jnp.bfloat16)


def draw_cache_len(key, part):
    key = jax.random.fold_in(key, 13)
    k_raw, k_dev, k_top = jax.random.split(key, 3)
    devices = SEQS // SEQ_DEV
    raw = jax.random.randint(k_raw, (SEQS,), 0, CACHE - 1)
    factor = jax.random.randint(k_dev, (devices,), 1, 5)
    owner = jnp.arange(SEQS) // SEQ_DEV
    length = 2 + raw * factor[owner] // 4
    longest = jax.random.randint(k_top, (), 0, SEQS)
    return jnp.where(jnp.arange(SEQS) == longest, CACHE, length).astype(jnp.int32)


def draw_expert_ids(key, part):
    key = jax.random.fold_in(key, 14)
    k_cnt, k_full, k_rank, k_other, k_turn = jax.random.split(key, 5)
    devices = SEQS // SEQ_DEV
    counts = jax.random.randint(k_cnt, (devices,), 1, CAP + 1)
    fullest = jax.random.randint(k_full, (), 0, devices)
    counts = jnp.where(jnp.arange(devices) == fullest, CAP, counts)
    scores = jax.random.randint(k_rank, (devices, SEQ_DEV), 0, 2 ** 20) * SEQ_DEV + jnp.arange(SEQ_DEV)[None, :]
    order = jnp.argsort(jnp.argsort(scores, axis=-1), axis=-1)
    routed = (order < counts[:, None]).reshape(SEQS)
    others = jax.random.randint(k_other, (SEQS, EXPERTS - 1), 0, 2 ** 20) * EXPERTS + jnp.arange(EXPERTS - 1)[None, :]
    picks = jnp.argsort(others, axis=-1)[:, :TOP] + 1
    with_zero = jnp.concatenate([jnp.zeros((SEQS, 1), jnp.int32), picks[:, :TOP - 1].astype(jnp.int32)], axis=1)
    ids = jnp.where(routed[:, None], with_zero, picks.astype(jnp.int32))
    turn = jax.random.randint(k_turn, (SEQS, 1), 0, TOP)
    index = (jnp.arange(TOP)[None, :] + turn) % TOP
    return jnp.take_along_axis(ids, index, axis=1).astype(jnp.int32)


def steps_of(own_key, shape, shards, low, high):
    def one(axis_at, blocks):
        steps = jax.random.uniform(jax.random.fold_in(jax.random.fold_in(own_key, 6), axis_at), (blocks,), jnp.float32, low / len(shards), high / len(shards))
        return jnp.repeat(jnp.exp(steps), shape[axis_at] // blocks).reshape((-1,) + (1,) * (len(shape) - axis_at - 1))

    level = one(*shards[0])
    for cut in shards[1:]:
        level = level * one(*cut)
    return level


def noise(stream_key, dims, spread, reach, cuts=(), dtype=jnp.bfloat16):
    factor_of = steps_of(stream_key, dims, cuts, -0.22, 0.18) if cuts else 1.0
    drawn = jax.random.normal(stream_key, dims, jnp.float32) * spread * factor_of
    return jnp.minimum(jnp.maximum(drawn, -reach), reach).astype(dtype)


def setup_inputs(seed: int = 0, part: int = 0) -> dict:
    seeds = jax.random.split(jax.random.key(seed), 13)
    part_splits = jax.random.split(jax.random.fold_in(seeds[12], part), 13)
    query = draw_query(jax.random.fold_in(jax.random.fold_in(seeds[12], part), 71), part)
    new_kv = noise(part_splits[1], (SEQS, 2, KV_HEADS * HEAD), 1.0, 6.0, ((0, 16),))
    cache_kv = draw_cache_kv(jax.random.fold_in(jax.random.fold_in(seeds[12], part), 71), part)
    cache_len = draw_cache_len(jax.random.fold_in(jax.random.fold_in(seeds[12], part), 71), part)
    prefix_kv = noise(part_splits[4], (PREFIX, 2, KV_HEADS * HEAD), 1.0, 6.0, ((0, 16),))
    residual_in = noise(part_splits[5], (SEQS, D), 0.05, 0.29882812, ((0, 16),))
    norm_gain = jnp.clip(1.0 + 0.15 * jax.random.normal(seeds[6], (D,), jnp.float32), 0.25, 1.75)
    router_w = noise(seeds[7], (D, EXPERTS), (D / 9) ** -0.5, 0.21875)
    expert_ids = draw_expert_ids(jax.random.fold_in(jax.random.fold_in(seeds[12], part), 71), part)
    w_gate = noise(seeds[9], (D, FF), D ** -0.5, 0.078125, ((1, 16),))
    w_up = noise(seeds[10], (D, FF), D ** -0.5, 0.078125, ((1, 16),))
    w_down = noise(seeds[11], (FF, D), (FF / 4) ** -0.5, 0.125, ((0, 16),))
    return {"query": query, "new_kv": new_kv, "cache_kv": cache_kv, "cache_len": cache_len, "prefix_kv": prefix_kv, "residual_in": residual_in, "norm_gain": norm_gain, "router_w": router_w, "expert_ids": expert_ids, "w_gate": w_gate, "w_up": w_up, "w_down": w_down}


def attend_one(args, prefix_kv):
    query, cache_kv, length, new_kv = args
    group = HEADS // KV_HEADS
    q32 = query.astype(jnp.float32).reshape(KV_HEADS, group, HEAD)
    keys = jnp.concatenate([prefix_kv[:, 0], cache_kv[0], new_kv[0][None]], axis=0)
    values = jnp.concatenate([prefix_kv[:, 1], cache_kv[1], new_kv[1][None]], axis=0)
    count = keys.shape[0]
    k32 = keys.astype(jnp.float32).reshape(count, KV_HEADS, HEAD)
    v32 = values.astype(jnp.float32).reshape(count, KV_HEADS, HEAD)
    scores = jnp.einsum('grd,mgd->grm', q32, k32) * HEAD ** (-0.5)
    position = jnp.arange(count) - PREFIX
    live = (position < 0) | (position < length) | (position == CACHE)
    masked = jnp.where(live[None, None, :], scores, -1e+30)
    top = lax.optimization_barrier(jnp.max(masked, axis=-1, keepdims=True))
    expo = jnp.where(live[None, None, :], jnp.exp(masked - top), 0.0)
    den = lax.optimization_barrier(jnp.sum(expo, axis=-1))
    probs = expo.astype(jnp.bfloat16).astype(jnp.float32)
    num = jnp.einsum('grm,mgd->grd', probs, v32)
    return (num / den[..., None]).reshape(HEADS * HEAD).astype(jnp.bfloat16)

def reference(query, new_kv, cache_kv, cache_len, prefix_kv, residual_in, norm_gain, router_w, expert_ids, w_gate, w_up, w_down):
    attn = lax.map(lambda a: attend_one(a, prefix_kv), (query, cache_kv, cache_len.astype(jnp.int32), new_kv))
    hidden = residual_in.astype(jnp.float32) + attn.astype(jnp.float32)
    meansq = lax.optimization_barrier(jnp.mean(hidden * hidden, axis=-1, keepdims=True))
    normed = (hidden * lax.rsqrt(meansq + 1e-05) * norm_gain).astype(jnp.bfloat16)
    logits = jnp.dot(normed, router_w, preferred_element_type=jnp.float32)
    router = jax.nn.softmax(logits, axis=-1)
    chosen = (expert_ids[:, :, None] == jnp.arange(EXPERTS)[None, None, :]).astype(jnp.float32)
    picked = lax.optimization_barrier(jnp.sum(router[:, None, :] * chosen, axis=(1, 2)))
    routed = jnp.any(expert_ids == 0, axis=-1)
    weight = jnp.where(routed, router[:, 0], 0.0) / picked
    gate = jnp.dot(normed, w_gate, preferred_element_type=jnp.float32)
    upper = jnp.dot(normed, w_up, preferred_element_type=jnp.float32)
    inner = (jax.nn.silu(gate) * upper).astype(jnp.bfloat16)
    expert_out = jnp.dot(inner, w_down, preferred_element_type=jnp.float32)
    return (hidden + weight[:, None] * expert_out).astype(jnp.bfloat16)
```

```python
import functools

import jax
import jax.numpy as jnp
from jax import lax
from jax.experimental import pallas as pl
from jax.experimental.pallas import tpu as pltpu
from jax.sharding import PartitionSpec as P

HEADS = 48
KV_HEADS = 8
GROUP = HEADS // KV_HEADS
HEAD = 128
EXPERTS = 16
TOP = 4
CACHE = 128
CAP = 4
CUTS = 4
NEG = -1e30
F32 = jnp.float32
BF16 = jnp.bfloat16
NT = (((1,), (1,)), ((), ()))
NN = (((1,), (0,)), ((), ()))


def mm(a, b, dims=NN):
    return lax.dot_general(a, b, dims, preferred_element_type=F32)


def iota(shape, dim):
    return lax.broadcasted_iota(jnp.int32, shape, dim)


def kernel(
    n,
    query,
    new_kv,
    cache_hbm,
    lens,
    prefix,
    residual,
    gain,
    router_w,
    ids,
    wg_hbm,
    wu_hbm,
    wd_hbm,
    out,
    cache,
    wg,
    wu,
    wd,
    pbuf,
    q32,
    acc_ref,
    top_ref,
    den_ref,
    hidden_ref,
    xbuf,
    xs,
    inner_ref,
    ystack,
    msg,
    got_core,
    sum_core,
    got_y,
    sum_y,
    got_z,
    fetch,
    psend,
    precv,
    xsend,
    xrecv,
    csend,
    crecv,
    ysend,
    yrecv,
    zsend,
    zrecv,
):
    seqs = query.shape[0]
    d = query.shape[1]
    ff = wg.shape[0]
    hi_n = n // 4
    rows = seqs * GROUP
    wide = d // CUTS
    thin = wide // CUTS
    factor = HEAD ** (-0.5)
    me = lax.axis_index("node")
    core = lax.rem(me, 2)
    yy = lax.rem(me // 2, 2)
    hi = me // 4
    core_peer = hi * 4 + yy * 2 + (1 - core)
    y_peer = hi * 4 + (1 - yy) * 2 + core

    def z_peer(k):
        return lax.rem(hi + k, hi_n) * 4 + yy * 2 + core

    def place(h, y, c):
        return c * (n // 2) + y * hi_n + h

    slot = place(hi, yy, core)

    def remote(src, dst, ssem, rsem, dev):
        return pltpu.make_async_remote_copy(
            src_ref=src,
            dst_ref=dst,
            send_sem=ssem,
            recv_sem=rsem,
            device_id={"node": dev},
            device_id_type=pl.DeviceIdType.MESH,
        )

    loads = [
        pltpu.make_async_copy(cache_hbm, cache, fetch.at[0]),
        pltpu.make_async_copy(wg_hbm, wg, fetch.at[1]),
        pltpu.make_async_copy(wu_hbm, wu, fetch.at[2]),
        pltpu.make_async_copy(wd_hbm, wd, fetch.at[3]),
    ]
    for load in loads:
        load.start()

    barrier = pltpu.get_barrier_semaphore()
    partners = [core_peer, y_peer] + [z_peer(k) for k in range(1, hi_n)]
    for dev in partners:
        pl.semaphore_signal(
            barrier, inc=1, device_id={"node": dev}, device_id_type=pl.DeviceIdType.MESH
        )

    pbuf[slot, 0] = prefix[:, 0, :]
    pbuf[slot, 1] = prefix[:, 1, :]
    nkv = new_kv[...].astype(F32)
    new_key = nkv[:, 0, :]
    new_val = nkv[:, 1, :]
    q32[...] = query[...].astype(F32)

    pl.semaphore_wait(barrier, len(partners))

    def hop_z(buf, ssem, rsem):
        return [
            remote(buf.at[slot], buf.at[slot], ssem.at[k - 1], rsem.at[slot], z_peer(k))
            for k in range(1, hi_n)
        ]

    def hop_y(buf, ssem, rsem, k):
        at = place(lax.rem(hi + k, hi_n), yy, core)
        return remote(buf.at[at], buf.at[at], ssem.at[hi_n - 1 + k], rsem.at[at], y_peer)

    def hop_core(buf, ssem, rsem, k, side):
        h = lax.rem(hi + k, hi_n)
        y = yy if side == 0 else 1 - yy
        at = place(h, y, core)
        return remote(
            buf.at[at],
            buf.at[at],
            ssem.at[2 * hi_n - 1 + side * hi_n + k],
            rsem.at[at],
            core_peer,
        )

    def arrive(buf, rsem, at):
        pltpu.make_async_copy(buf.at[at], buf.at[at], rsem.at[at]).wait()

    class Gather:
        def __init__(self, buf, ssem, rsem):
            self.args = (buf, ssem, rsem)
            self.sent = []

        def go(self, copy):
            copy.start()
            self.sent.append(copy)

        def first(self):
            for copy in hop_z(*self.args):
                self.go(copy)
            self.go(hop_y(*self.args, 0))
            self.go(hop_core(*self.args, 0, 0))

        def from_z(self, k):
            arrive(self.args[0], self.args[2], place(lax.rem(hi + k, hi_n), yy, core))
            self.go(hop_y(*self.args, k))
            self.go(hop_core(*self.args, k, 0))

        def from_y(self, k):
            arrive(self.args[0], self.args[2], place(lax.rem(hi + k, hi_n), 1 - yy, core))
            self.go(hop_core(*self.args, k, 1))

        def from_core(self):
            for y in range(2):
                for h in range(hi_n):
                    arrive(self.args[0], self.args[2], place(h, y, 1 - core))

        def drain(self):
            for copy in self.sent:
                copy.wait_send()

    pre = Gather(pbuf, psend, precv)
    pre.first()

    eye = iota((seqs, seqs), 0) == iota((seqs, seqs), 1)

    def column(row):
        return jnp.sum(jnp.where(eye, jnp.broadcast_to(row, (seqs, seqs)), 0.0), axis=1, keepdims=True)

    len_col = column(lens[...].astype(F32))
    live = iota((seqs, CACHE), 1).astype(F32) < len_col
    live = jnp.concatenate([live.astype(F32)] * GROUP, axis=0) > 0.0
    srow = lax.rem(iota((rows, CACHE), 0), seqs)
    loads[0].wait()

    def queries(g):
        return jnp.concatenate(
            [q32[:, (g * GROUP + r) * HEAD : (g * GROUP + r + 1) * HEAD] for r in range(GROUP)], axis=0
        )

    for g in range(KV_HEADS):
        lanes = slice(g * HEAD, (g + 1) * HEAD)
        q = queries(g)
        qb = q.astype(BF16)
        s = jnp.zeros((rows, CACHE), F32)
        for t in range(seqs):
            s = jnp.where(srow == t, mm(qb, cache[t, 0, :, lanes], NT), s)
        s = jnp.where(live, s * factor, NEG)
        nk = jnp.concatenate([new_key[:, lanes]] * GROUP, axis=0)
        own = jnp.sum(q * nk, axis=1, keepdims=True) * factor
        top = jnp.maximum(jnp.max(s, axis=1, keepdims=True), own)
        e = jnp.where(live, jnp.exp(s - top), 0.0)
        e_own = jnp.exp(own - top)
        den = jnp.sum(e, axis=1, keepdims=True) + e_own
        nv = jnp.concatenate([new_val[:, lanes]] * GROUP, axis=0)
        acc = e_own.astype(BF16).astype(F32) * nv
        for t in range(seqs):
            acc = acc + mm(jnp.where(srow == t, e, 0.0).astype(BF16), cache[t, 1, :, lanes])
        acc_ref[g] = acc
        top_ref[g] = jnp.broadcast_to(top, (rows, HEAD))
        den_ref[g] = jnp.broadcast_to(den, (rows, HEAD))
        if g == 5:
            for k in range(1, hi_n):
                pre.from_z(k)
    for k in range(hi_n):
        pre.from_y(k)
    pre.from_core()

    count = n * prefix.shape[0]
    square = jnp.zeros((seqs, HEAD), F32)
    for g in range(KV_HEADS):
        lanes = slice(g * HEAD, (g + 1) * HEAD)
        qb = queries(g).astype(BF16)
        keys = pbuf[:, 0, :, lanes].reshape(count, HEAD)
        vals = pbuf[:, 1, :, lanes].reshape(count, HEAD)
        s = mm(qb, keys, NT) * factor
        best = top_ref[g][:, :1]
        top = jnp.maximum(best, jnp.max(s, axis=1, keepdims=True))
        shrink = jnp.exp(best - top)
        e = jnp.exp(s - top)
        den = den_ref[g][:, :1] * shrink + jnp.sum(e, axis=1, keepdims=True)
        acc = acc_ref[g] * shrink + mm(e.astype(BF16), vals)
        attn = (acc / den).astype(BF16).astype(F32)
        for r in range(GROUP):
            at = slice((g * GROUP + r) * HEAD, (g * GROUP + r + 1) * HEAD)
            h = residual[:, at].astype(F32) + attn[r * seqs : (r + 1) * seqs]
            hidden_ref[:, at] = h
            square = square + h * h

    scale = lax.rsqrt(jnp.sum(square, axis=1, keepdims=True) / d + 1e-5)
    normed = (hidden_ref[...] * scale * gain[...]).astype(BF16)

    routed_row = jnp.zeros((1, seqs), F32)
    for j in range(TOP):
        routed_row = jnp.maximum(routed_row, (ids[j : j + 1, :] == 0).astype(F32))
    routed_col = column(routed_row)
    before = jnp.where(iota((seqs, seqs), 0) < iota((seqs, seqs), 1), routed_col, 0.0)
    rank_row = jnp.sum(before, axis=0, keepdims=True)
    packed = jnp.zeros((CAP * CUTS, wide), F32)
    for c in range(CUTS):
        at = (iota((CAP * CUTS, seqs), 0) - CAP * c).astype(F32)
        pick = jnp.where((at == rank_row) & (routed_row > 0.0), 1.0, 0.0).astype(BF16)
        packed = packed + mm(pick, normed[:, c * wide : (c + 1) * wide])
    xbuf[slot] = packed.astype(BF16)

    tok = Gather(xbuf, xsend, xrecv)
    tok.first()

    logits = mm(normed, router_w[...], NT)
    expo = jnp.exp(logits - jnp.max(logits, axis=1, keepdims=True))
    router = expo / jnp.sum(expo, axis=1, keepdims=True)
    expert = iota((seqs, EXPERTS), 1).astype(F32)
    chosen = jnp.zeros((seqs, EXPERTS), F32)
    for j in range(TOP):
        chosen = chosen + (expert == column(ids[j : j + 1, :].astype(F32))).astype(F32)
    picked = jnp.sum(router * chosen, axis=1, keepdims=True)
    weight = jnp.where(routed_col > 0.0, router[:, :1], 0.0) / picked
    rank_col = column(rank_row)

    size = CAP * n
    across = CAP * CUTS * n
    a = iota((across, across), 0)
    b = iota((across, across), 1)
    def packed_row(x):
        return CAP * CUTS * (lax.rem(x, size) // CAP) + CAP * (x // size) + lax.rem(x, CAP)

    to_stack = (packed_row(a) == b).astype(F32).astype(BF16)
    to_pack = (packed_row(b) == a).astype(F32).astype(BF16)

    for k in range(1, hi_n):
        tok.from_z(k)
    for k in range(hi_n):
        tok.from_y(k)
    tok.from_core()

    xs[...] = mm(to_stack, xbuf[...].reshape(across, wide)).astype(BF16)

    loads[1].wait()
    loads[2].wait()
    gate = jnp.zeros((size, ff), F32)
    upper = jnp.zeros((size, ff), F32)
    for c in range(CUTS):
        x = xs[c * size : (c + 1) * size, :]
        gate = gate + mm(x, wg[:, c * wide : (c + 1) * wide], NT)
        upper = upper + mm(x, wu[:, c * wide : (c + 1) * wide], NT)
    inner_ref[...] = (gate / (1.0 + jnp.exp(-gate)) * upper).astype(BF16)

    loads[3].wait()
    half = n // 2

    def hop1(c):
        src = msg.at[c, pl.ds((1 - core) * half, half)]
        return remote(src, got_core.at[c], csend.at[c], crecv.at[c], core_peer)

    def hop2(c):
        src = sum_core.at[c, pl.ds((1 - yy) * hi_n, hi_n)]
        return remote(src, got_y.at[c], ysend.at[c], yrecv.at[c], y_peer)

    def hop3(c, k):
        h = lax.rem(hi + k, hi_n)
        return remote(
            sum_y.at[c, h], got_z.at[c, k - 1], zsend.at[c, k - 1], zrecv.at[c, k - 1], z_peer(k)
        )

    def work(c):
        inner = inner_ref[...]
        for piece in range(CUTS):
            lo = c * wide + piece * thin
            ystack[c, piece * size : (piece + 1) * size, :] = mm(inner, wd[:, lo : lo + thin]).astype(BF16)
        full = mm(to_pack, ystack[c]).astype(BF16)
        msg[c] = full.reshape(n, CAP * CUTS, thin)
        hop1(c).start()

    def add_core(c):
        hop1(c).wait_recv()
        total = msg[c, pl.ds(core * half, half)].astype(F32) + got_core[c].astype(F32)
        sum_core[c] = total.astype(BF16)
        hop2(c).start()

    def add_y(c):
        hop2(c).wait_recv()
        total = sum_core[c, pl.ds(yy * hi_n, hi_n)].astype(F32) + got_y[c].astype(F32)
        sum_y[c] = total.astype(BF16)
        for k in range(1, hi_n):
            hop3(c, k).start()

    def finish(c):
        total = sum_y[c, hi].astype(F32)
        for k in range(1, hi_n):
            hop3(c, k).wait_recv()
            total = total + got_z[c, k - 1].astype(F32)
        for piece in range(CUTS):
            lo = c * wide + piece * thin
            y = jnp.zeros((seqs, thin), F32)
            for k in range(CAP):
                mine = (rank_col == float(k)) & (routed_col > 0.0)
                at = piece * CAP + k
                y = y + jnp.where(mine, total[at : at + 1, :], 0.0)
            out[:, lo : lo + thin] = (hidden_ref[:, lo : lo + thin] + weight * y).astype(BF16)

    for step in range(CUTS + 3):
        if step < CUTS:
            work(step)
        if 0 <= step - 1 < CUTS:
            add_core(step - 1)
        if 0 <= step - 2 < CUTS:
            add_y(step - 2)
        if 0 <= step - 3 < CUTS:
            finish(step - 3)

    pre.drain()
    tok.drain()
    for c in range(CUTS):
        hop1(c).wait_send()
        hop2(c).wait_send()
        for k in range(1, hi_n):
            hop3(c, k).wait_send()


def body(n, query, new_kv, cache_kv, cache_len, prefix_kv, residual_in, norm_gain, router_w, expert_ids, w_gate, w_up, w_down):
    seqs, d = query.shape
    ff = w_down.shape[0]
    per = prefix_kv.shape[0]
    width = KV_HEADS * HEAD
    rows = seqs * GROUP
    wide = d // CUTS
    thin = wide // CUTS
    packs = CAP * CUTS
    hi_n = n // 4
    hops = max(hi_n - 1, 1)
    vmem = pl.BlockSpec(memory_space=pltpu.VMEM)
    hbm = pl.BlockSpec(memory_space=pl.ANY)
    dma = pltpu.SemaphoreType.DMA
    sends = 4 * hi_n - 1
    return pl.pallas_call(
        functools.partial(kernel, n),
        out_shape=jax.ShapeDtypeStruct((seqs, d), BF16),
        in_specs=[vmem, vmem, hbm, vmem, vmem, vmem, vmem, vmem, vmem, hbm, hbm, hbm],
        out_specs=vmem,
        scratch_shapes=[
            pltpu.VMEM((seqs, 2, CACHE, width), BF16),
            pltpu.VMEM((ff, d), BF16),
            pltpu.VMEM((ff, d), BF16),
            pltpu.VMEM((ff, d), BF16),
            pltpu.VMEM((n, 2, per, width), BF16),
            pltpu.VMEM((seqs, d), F32),
            pltpu.VMEM((KV_HEADS, rows, HEAD), F32),
            pltpu.VMEM((KV_HEADS, rows, HEAD), F32),
            pltpu.VMEM((KV_HEADS, rows, HEAD), F32),
            pltpu.VMEM((seqs, d), F32),
            pltpu.VMEM((n, packs, wide), BF16),
            pltpu.VMEM((n * packs, wide), BF16),
            pltpu.VMEM((CAP * n, ff), BF16),
            pltpu.VMEM((CUTS, n * packs, thin), BF16),
            pltpu.VMEM((CUTS, n, packs, thin), BF16),
            pltpu.VMEM((CUTS, n // 2, packs, thin), BF16),
            pltpu.VMEM((CUTS, n // 2, packs, thin), BF16),
            pltpu.VMEM((CUTS, hi_n, packs, thin), BF16),
            pltpu.VMEM((CUTS, hi_n, packs, thin), BF16),
            pltpu.VMEM((CUTS, hops, packs, thin), BF16),
            dma((4,)),
            dma((sends,)),
            dma((n,)),
            dma((sends,)),
            dma((n,)),
            dma((CUTS,)),
            dma((CUTS,)),
            dma((CUTS,)),
            dma((CUTS,)),
            dma((CUTS, hops)),
            dma((CUTS, hops)),
        ],
        compiler_params=pltpu.CompilerParams(
            collective_id=0, has_side_effects=True, vmem_limit_bytes=60 * 1024 * 1024
        ),
        cost_estimate=pl.CostEstimate(
            flops=6 * CAP * n * d * ff, bytes_accessed=6 * d * ff + 2 * cache_kv.size, transcendentals=0
        ),
    )(
        query,
        new_kv,
        cache_kv,
        cache_len.reshape(1, seqs),
        prefix_kv,
        residual_in,
        norm_gain.reshape(1, d),
        router_w.T,
        expert_ids.T,
        w_gate.T,
        w_up.T,
        w_down,
    )


def solution(mesh):
    return jax.shard_map(
        functools.partial(body, mesh.shape["node"]),
        mesh=mesh,
        in_specs=(
            P(("groups", "node"), None),
            P(("groups", "node"), None, None),
            P(("groups", "node"), None, None, None),
            P(("groups", "node")),
            P(("groups", "node"), None, None),
            P(("groups", "node"), None),
            P(),
            P(),
            P(("groups", "node"), None),
            P(None, "node"),
            P(None, "node"),
            P("node", None),
        ),
        out_specs=P(("groups", "node"), None),
        check_vma=False,
    )
```

```python
import functools

import jax
import jax.numpy as jnp
from jax import lax
from jax.experimental import pallas as pl
from jax.experimental.pallas import tpu as pltpu
from jax.sharding import PartitionSpec as P

HEADS = 48
KV_HEADS = 8
GROUP = HEADS // KV_HEADS
HEAD = 128
EXPERTS = 16
TOP = 4
CACHE = 128
CAP = 4
CUTS = 4
NEG = -1e30
F32 = jnp.float32
BF16 = jnp.bfloat16
NT = (((1,), (1,)), ((), ()))
NN = (((1,), (0,)), ((), ()))


def mm(a, b, dims=NN):
    return lax.dot_general(a, b, dims, preferred_element_type=F32)


def iota(shape, dim):
    return lax.broadcasted_iota(jnp.int32, shape, dim)


def kernel(
    n,
    query_hbm,
    new_kv_hbm,
    cache_hbm,
    lens_hbm,
    prefix_hbm,
    residual_hbm,
    gain_hbm,
    router_hbm,
    ids_hbm,
    wg_hbm,
    wu_hbm,
    wd_hbm,
    out,
    query,
    new_kv,
    cache,
    lens,
    prefix,
    residual,
    gain,
    router_w,
    ids,
    wg,
    wu,
    wd,
    pbuf,
    q32,
    acc_ref,
    top_ref,
    den_ref,
    hidden_ref,
    xbuf,
    gate_ref,
    upper_ref,
    inner_ref,
    ystack,
    msg,
    got_core,
    sum_core,
    got_y,
    sum_y,
    got_z,
    fetch,
    pzs,
    pzr,
    pys,
    pyr,
    pcs,
    pcr,
    xzs,
    xzr,
    xys,
    xyr,
    xcs,
    xcr,
    csend,
    crecv,
    ysend,
    yrecv,
    zsend,
    zrecv,
):
    seqs, d = query.shape
    ff = wg.shape[0]
    hi_n = n // 4
    rows = seqs * GROUP
    wide = d // CUTS
    thin = wide // CUTS
    factor = HEAD ** (-0.5)
    me = lax.axis_index("node")
    core = lax.rem(me, 2)
    yy = lax.rem(me // 2, 2)
    hi = me // 4
    core_peer = hi * 4 + yy * 2 + (1 - core)
    y_peer = hi * 4 + (1 - yy) * 2 + core

    def z_peer(k):
        return lax.rem(hi + k, hi_n) * 4 + yy * 2 + core

    def place(h, y, c):
        return c * (n // 2) + y * hi_n + h

    slot = place(hi, yy, core)

    def remote(src, dst, ssem, rsem, dev):
        return pltpu.make_async_remote_copy(
            src_ref=src,
            dst_ref=dst,
            send_sem=ssem,
            recv_sem=rsem,
            device_id={"node": dev},
            device_id_type=pl.DeviceIdType.MESH,
        )

    barrier = pltpu.get_barrier_semaphore()
    partners = [core_peer, y_peer] + [z_peer(k) for k in range(1, hi_n)]
    for dev in partners:
        pl.semaphore_signal(
            barrier, inc=1, device_id={"node": dev}, device_id_type=pl.DeviceIdType.MESH
        )

    pairs = [
        (query_hbm, query),
        (lens_hbm, lens),
        (new_kv_hbm, new_kv),
        (cache_hbm, cache),
        (prefix_hbm, prefix),
        (residual_hbm, residual),
        (gain_hbm, gain),
        (ids_hbm, ids),
        (router_hbm, router_w),
        (wg_hbm, wg),
        (wu_hbm, wu),
        (wd_hbm, wd),
    ]
    loads = [pltpu.make_async_copy(a, b, fetch.at[i]) for i, (a, b) in enumerate(pairs)]
    for load in loads:
        load.start()

    half = n // 2
    line = core * half + yy * hi_n
    other = core * half + (1 - yy) * hi_n

    class Gather:
        def __init__(self, buf, zs, zr, ys, yr, cs, cr):
            self.buf = buf
            self.sems = (zs, zr, ys, yr, cs, cr)
            self.sent = []

        def go(self, src, ssem, rsem, dev):
            copy = remote(src, src, ssem, rsem, dev)
            copy.start()
            self.sent.append(copy)

        def arrive(self, ref, sem):
            pltpu.make_async_copy(ref, ref, sem).wait()

        def first(self, c):
            zs, zr = self.sems[:2]
            for k in range(1, hi_n):
                self.go(self.buf.at[c, slot], zs.at[c, k - 1], zr.at[c, k - 1], z_peer(k))

        def from_z(self, c):
            zs, zr, ys, yr, cs, cr = self.sems
            for k in range(1, hi_n):
                at = place(lax.rem(hi + hi_n - k, hi_n), yy, core)
                self.arrive(self.buf.at[c, at], zr.at[c, k - 1])
            mine = self.buf.at[c, pl.ds(line, hi_n)]
            self.go(mine, ys.at[c], yr.at[c], y_peer)
            self.go(mine, cs.at[c, 0], cr.at[c, 0], core_peer)

        def from_y(self, c):
            zs, zr, ys, yr, cs, cr = self.sems
            ref = self.buf.at[c, pl.ds(other, hi_n)]
            self.arrive(ref, yr.at[c])
            self.go(ref, cs.at[c, 1], cr.at[c, 1], core_peer)

        def from_core(self, c):
            cr = self.sems[5]
            for side, y in ((0, yy), (1, 1 - yy)):
                ref = self.buf.at[c, pl.ds((1 - core) * half + y * hi_n, hi_n)]
                self.arrive(ref, cr.at[c, side])

        def drain(self):
            for copy in self.sent:
                copy.wait_send()

        def run(self, use):
            for c in range(CUTS):
                self.from_z(c)
            self.from_y(0)
            for c in range(CUTS):
                if c + 1 < CUTS:
                    self.from_y(c + 1)
                self.from_core(c)
                use(c)

    for at in range(3):
        loads[at].wait()
    nkv = new_kv[...].astype(F32)
    new_key = nkv[:, 0, :]
    new_val = nkv[:, 1, :]
    q32[...] = query[...].astype(F32)

    eye = iota((seqs, seqs), 0) == iota((seqs, seqs), 1)

    def column(row):
        return jnp.sum(jnp.where(eye, jnp.broadcast_to(row, (seqs, seqs)), 0.0), axis=1, keepdims=True)

    len_col = column(lens[...].astype(F32))
    live = iota((seqs, CACHE), 1).astype(F32) < len_col
    live = jnp.concatenate([live.astype(F32)] * GROUP, axis=0) > 0.0
    srow = lax.rem(iota((rows, CACHE), 0), seqs)
    loads[3].wait()

    def queries(g):
        return jnp.concatenate(
            [q32[:, (g * GROUP + r) * HEAD : (g * GROUP + r + 1) * HEAD] for r in range(GROUP)], axis=0
        )

    for g in range(KV_HEADS):
        lanes = slice(g * HEAD, (g + 1) * HEAD)
        q = queries(g)
        qb = q.astype(BF16)
        s = jnp.zeros((rows, CACHE), F32)
        for t in range(seqs):
            s = jnp.where(srow == t, mm(qb, cache[t, 0, :, lanes], NT), s)
        s = jnp.where(live, s * factor, NEG)
        nk = jnp.concatenate([new_key[:, lanes]] * GROUP, axis=0)
        own = jnp.sum(q * nk, axis=1, keepdims=True) * factor
        top = jnp.maximum(jnp.max(s, axis=1, keepdims=True), own)
        e = jnp.where(live, jnp.exp(s - top), 0.0)
        e_own = jnp.exp(own - top)
        den = jnp.sum(e, axis=1, keepdims=True) + e_own
        nv = jnp.concatenate([new_val[:, lanes]] * GROUP, axis=0)
        acc = e_own.astype(BF16).astype(F32) * nv
        for t in range(seqs):
            acc = acc + mm(jnp.where(srow == t, e, 0.0).astype(BF16), cache[t, 1, :, lanes])
        acc_ref[g] = acc
        top_ref[g] = jnp.broadcast_to(top, (rows, HEAD))
        den_ref[g] = jnp.broadcast_to(den, (rows, HEAD))

    loads[4].wait()
    span = KV_HEADS // CUTS * HEAD
    for c in range(CUTS):
        for kv in range(2):
            pbuf[c, slot, kv] = prefix[:, kv, c * span : (c + 1) * span]
    for at in range(5, 9):
        loads[at].wait()

    pl.semaphore_wait(barrier, len(partners))
    pre = Gather(pbuf, pzs, pzr, pys, pyr, pcs, pcr)
    for c in range(CUTS):
        pre.first(c)

    count = n * prefix.shape[0]
    square = [jnp.zeros((seqs, HEAD), F32)]

    def attend(c):
        for part in range(KV_HEADS // CUTS):
            g = c * (KV_HEADS // CUTS) + part
            lanes = slice(part * HEAD, (part + 1) * HEAD)
            qb = queries(g).astype(BF16)
            keys = pbuf[c, :, 0, :, lanes].reshape(count, HEAD)
            vals = pbuf[c, :, 1, :, lanes].reshape(count, HEAD)
            s = mm(qb, keys, NT) * factor
            best = top_ref[g][:, :1]
            top = jnp.maximum(best, jnp.max(s, axis=1, keepdims=True))
            shrink = jnp.exp(best - top)
            e = jnp.exp(s - top)
            den = den_ref[g][:, :1] * shrink + jnp.sum(e, axis=1, keepdims=True)
            acc = acc_ref[g] * shrink + mm(e.astype(BF16), vals)
            attn = (acc / den).astype(BF16).astype(F32)
            for r in range(GROUP):
                at = slice((g * GROUP + r) * HEAD, (g * GROUP + r + 1) * HEAD)
                h = residual[:, at].astype(F32) + attn[r * seqs : (r + 1) * seqs]
                hidden_ref[:, at] = h
                square[0] = square[0] + h * h

    pre.run(attend)
    square = square[0]

    scale = lax.rsqrt(jnp.sum(square, axis=1, keepdims=True) / d + 1e-5)
    normed = (hidden_ref[...] * scale * gain[...]).astype(BF16)

    routed_row = jnp.zeros((1, seqs), F32)
    for j in range(TOP):
        routed_row = jnp.maximum(routed_row, (ids[j : j + 1, :] == 0).astype(F32))
    routed_col = column(routed_row)
    before = jnp.where(iota((seqs, seqs), 0) < iota((seqs, seqs), 1), routed_col, 0.0)
    rank_row = jnp.sum(before, axis=0, keepdims=True)
    picks = []
    for p in range(CUTS):
        at = (iota((CAP * CUTS, seqs), 0) - CAP * p).astype(F32)
        picks.append(jnp.where((at == rank_row) & (routed_row > 0.0), 1.0, 0.0).astype(BF16))
    tok = Gather(xbuf, xzs, xzr, xys, xyr, xcs, xcr)
    for c in range(CUTS):
        packed = jnp.zeros((CAP * CUTS, thin), F32)
        for p in range(CUTS):
            lo = c * wide + p * thin
            packed = packed + mm(picks[p], normed[:, lo : lo + thin])
        xbuf[c, slot] = packed.astype(BF16)
        tok.first(c)

    logits = mm(normed, router_w[...], NT)
    expo = jnp.exp(logits - jnp.max(logits, axis=1, keepdims=True))
    router = expo / jnp.sum(expo, axis=1, keepdims=True)
    expert = iota((seqs, EXPERTS), 1).astype(F32)
    chosen = jnp.zeros((seqs, EXPERTS), F32)
    for j in range(TOP):
        chosen = chosen + (expert == column(ids[j : j + 1, :].astype(F32))).astype(F32)
    picked = jnp.sum(router * chosen, axis=1, keepdims=True)
    weight = jnp.where(routed_col > 0.0, router[:, :1], 0.0) / picked
    rank_col = column(rank_row)

    size = CAP * n
    across = CAP * CUTS * n
    a = iota((across, across), 0)
    b = iota((across, across), 1)
    def packed_row(x):
        return CAP * CUTS * (lax.rem(x, size) // CAP) + CAP * (x // size) + lax.rem(x, CAP)

    to_stack = (packed_row(a) == b).astype(F32).astype(BF16)
    to_pack = (packed_row(b) == a).astype(F32).astype(BF16)

    loads[9].wait()
    loads[10].wait()

    def gate_up(c):
        stacked = mm(to_stack, xbuf[c].reshape(across, thin)).astype(BF16)
        x = jnp.concatenate([stacked[p * size : (p + 1) * size] for p in range(CUTS)], axis=1)
        gate = mm(x, wg[:, c * wide : (c + 1) * wide], NT)
        upper = mm(x, wu[:, c * wide : (c + 1) * wide], NT)
        if c:
            gate = gate + gate_ref[...]
            upper = upper + upper_ref[...]
        if c < CUTS - 1:
            gate_ref[...] = gate
            upper_ref[...] = upper
        else:
            inner_ref[...] = (gate / (1.0 + jnp.exp(-gate)) * upper).astype(BF16)

    tok.run(gate_up)

    loads[11].wait()

    def hop1(c):
        src = msg.at[c, pl.ds((1 - core) * half, half)]
        return remote(src, got_core.at[c], csend.at[c], crecv.at[c], core_peer)

    def hop2(c):
        src = sum_core.at[c, pl.ds((1 - yy) * hi_n, hi_n)]
        return remote(src, got_y.at[c], ysend.at[c], yrecv.at[c], y_peer)

    def hop3(c, k):
        h = lax.rem(hi + k, hi_n)
        return remote(
            sum_y.at[c, h], got_z.at[c, k - 1], zsend.at[c, k - 1], zrecv.at[c, k - 1], z_peer(k)
        )

    def work(c):
        inner = inner_ref[...]
        for piece in range(CUTS):
            lo = c * wide + piece * thin
            ystack[c, piece * size : (piece + 1) * size, :] = mm(inner, wd[:, lo : lo + thin]).astype(BF16)
        full = mm(to_pack, ystack[c]).astype(BF16)
        msg[c] = full.reshape(n, CAP * CUTS, thin)
        hop1(c).start()

    def add_core(c):
        hop1(c).wait_recv()
        total = msg[c, pl.ds(core * half, half)].astype(F32) + got_core[c].astype(F32)
        sum_core[c] = total.astype(BF16)
        hop2(c).start()

    def add_y(c):
        hop2(c).wait_recv()
        total = sum_core[c, pl.ds(yy * hi_n, hi_n)].astype(F32) + got_y[c].astype(F32)
        sum_y[c] = total.astype(BF16)
        for k in range(1, hi_n):
            hop3(c, k).start()

    def finish(c):
        total = sum_y[c, hi].astype(F32)
        for k in range(1, hi_n):
            hop3(c, k).wait_recv()
            total = total + got_z[c, k - 1].astype(F32)
        for piece in range(CUTS):
            lo = c * wide + piece * thin
            y = jnp.zeros((seqs, thin), F32)
            for k in range(CAP):
                mine = (rank_col == float(k)) & (routed_col > 0.0)
                at = piece * CAP + k
                y = y + jnp.where(mine, total[at : at + 1, :], 0.0)
            out[:, lo : lo + thin] = (hidden_ref[:, lo : lo + thin] + weight * y).astype(BF16)

    work(0)
    for c in range(1, CUTS):
        work(c)
        add_core(c - 1)
    add_core(CUTS - 1)
    for c in range(CUTS):
        add_y(c)
    for c in range(CUTS):
        finish(c)

    pre.drain()
    tok.drain()
    for c in range(CUTS):
        hop1(c).wait_send()
        hop2(c).wait_send()
        for k in range(1, hi_n):
            hop3(c, k).wait_send()


def body(n, query, new_kv, cache_kv, cache_len, prefix_kv, residual_in, norm_gain, router_w, expert_ids, w_gate, w_up, w_down):
    seqs, d = query.shape
    ff = w_down.shape[0]
    per = prefix_kv.shape[0]
    width = KV_HEADS * HEAD
    rows = seqs * GROUP
    wide = d // CUTS
    thin = wide // CUTS
    packs = CAP * CUTS
    hi_n = n // 4
    hops = max(hi_n - 1, 1)
    vmem = pl.BlockSpec(memory_space=pltpu.VMEM)
    hbm = pl.BlockSpec(memory_space=pl.ANY)
    dma = pltpu.SemaphoreType.DMA
    return pl.pallas_call(
        functools.partial(kernel, n),
        out_shape=jax.ShapeDtypeStruct((seqs, d), BF16),
        in_specs=[hbm] * 12,
        out_specs=vmem,
        scratch_shapes=[
            pltpu.VMEM((seqs, d), BF16),
            pltpu.VMEM((seqs, 2, width), BF16),
            pltpu.VMEM((seqs, 2, CACHE, width), BF16),
            pltpu.VMEM((1, seqs), jnp.int32),
            pltpu.VMEM((per, 2, width), BF16),
            pltpu.VMEM((seqs, d), BF16),
            pltpu.VMEM((1, d), F32),
            pltpu.VMEM((EXPERTS, d), BF16),
            pltpu.VMEM((TOP, seqs), jnp.int32),
            pltpu.VMEM((ff, d), BF16),
            pltpu.VMEM((ff, d), BF16),
            pltpu.VMEM((ff, d), BF16),
            pltpu.VMEM((CUTS, n, 2, per, width // CUTS), BF16),
            pltpu.VMEM((seqs, d), F32),
            pltpu.VMEM((KV_HEADS, rows, HEAD), F32),
            pltpu.VMEM((KV_HEADS, rows, HEAD), F32),
            pltpu.VMEM((KV_HEADS, rows, HEAD), F32),
            pltpu.VMEM((seqs, d), F32),
            pltpu.VMEM((CUTS, n, packs, thin), BF16),
            pltpu.VMEM((CAP * n, ff), F32),
            pltpu.VMEM((CAP * n, ff), F32),
            pltpu.VMEM((CAP * n, ff), BF16),
            pltpu.VMEM((CUTS, n * packs, thin), BF16),
            pltpu.VMEM((CUTS, n, packs, thin), BF16),
            pltpu.VMEM((CUTS, n // 2, packs, thin), BF16),
            pltpu.VMEM((CUTS, n // 2, packs, thin), BF16),
            pltpu.VMEM((CUTS, hi_n, packs, thin), BF16),
            pltpu.VMEM((CUTS, hi_n, packs, thin), BF16),
            pltpu.VMEM((CUTS, hops, packs, thin), BF16),
            dma((12,)),
            dma((CUTS, hops)),
            dma((CUTS, hops)),
            dma((CUTS,)),
            dma((CUTS,)),
            dma((CUTS, 2)),
            dma((CUTS, 2)),
            dma((CUTS, hops)),
            dma((CUTS, hops)),
            dma((CUTS,)),
            dma((CUTS,)),
            dma((CUTS, 2)),
            dma((CUTS, 2)),
            dma((CUTS,)),
            dma((CUTS,)),
            dma((CUTS,)),
            dma((CUTS,)),
            dma((CUTS, hops)),
            dma((CUTS, hops)),
        ],
        compiler_params=pltpu.CompilerParams(
            collective_id=0, has_side_effects=True, vmem_limit_bytes=60 * 1024 * 1024
        ),
        cost_estimate=pl.CostEstimate(
            flops=6 * CAP * n * d * ff, bytes_accessed=6 * d * ff + 2 * cache_kv.size, transcendentals=0
        ),
    )(
        query,
        new_kv,
        cache_kv,
        cache_len.reshape(1, seqs),
        prefix_kv,
        residual_in,
        norm_gain.reshape(1, d),
        router_w.T,
        expert_ids.T,
        w_gate.T,
        w_up.T,
        w_down,
    )


def solution(mesh):
    return jax.shard_map(
        functools.partial(body, mesh.shape["node"]),
        mesh=mesh,
        in_specs=(
            P(("groups", "node"), None),
            P(("groups", "node"), None, None),
            P(("groups", "node"), None, None, None),
            P(("groups", "node")),
            P(("groups", "node"), None, None),
            P(("groups", "node"), None),
            P(),
            P(),
            P(("groups", "node"), None),
            P(None, "node"),
            P(None, "node"),
            P("node", None),
        ),
        out_specs=P(("groups", "node"), None),
        check_vma=False,
    )
```

```python
import functools

import jax
import jax.numpy as jnp
from jax import lax
from jax.experimental import pallas as pl
from jax.experimental.pallas import tpu as pltpu
from jax.sharding import PartitionSpec as P

HEADS = 48
KV_HEADS = 8
GROUP = HEADS // KV_HEADS
HEAD = 128
EXPERTS = 16
TOP = 4
CACHE = 128
CAP = 4
PCUTS = 4
CUTS = 6
PIECES = 4
NEG = -1e30
F32 = jnp.float32
BF16 = jnp.bfloat16
NT = (((1,), (1,)), ((), ()))
NN = (((1,), (0,)), ((), ()))


def mm(a, b, dims=NN):
    return lax.dot_general(a, b, dims, preferred_element_type=F32)


def iota(shape, dim):
    return lax.broadcasted_iota(jnp.int32, shape, dim)


def kernel(
    n,
    query_hbm,
    new_kv_hbm,
    cache_hbm,
    lens_hbm,
    prefix_hbm,
    residual_hbm,
    gain_hbm,
    router_hbm,
    ids_hbm,
    wg_hbm,
    wu_hbm,
    wd_hbm,
    out,
    query,
    new_kv,
    cache,
    lens,
    prefix,
    residual,
    gain,
    router_w,
    ids,
    wg,
    wu,
    wd,
    pbuf,
    q32,
    acc_ref,
    top_ref,
    den_ref,
    hidden_ref,
    xbuf,
    gate_ref,
    upper_ref,
    inner_ref,
    ystack,
    msg,
    got_core,
    sum_core,
    got_y,
    sum_y,
    got_z,
    fetch,
    pzs,
    pzr,
    pys,
    pyr,
    pcs,
    pcr,
    xzs,
    xzr,
    xys,
    xyr,
    xcs,
    xcr,
    csend,
    crecv,
    ysend,
    yrecv,
    zsend,
    zrecv,
):
    seqs, d = query.shape
    ff = wg.shape[0]
    hi_n = n // 4
    rows = seqs * GROUP
    wide = d // CUTS
    thin = wide // PIECES
    factor = HEAD ** (-0.5)
    me = lax.axis_index("node")
    core = lax.rem(me, 2)
    yy = lax.rem(me // 2, 2)
    hi = me // 4
    core_peer = hi * 4 + yy * 2 + (1 - core)
    y_peer = hi * 4 + (1 - yy) * 2 + core

    def z_peer(k):
        return lax.rem(hi + k, hi_n) * 4 + yy * 2 + core

    def place(h, y, c):
        return c * (n // 2) + y * hi_n + h

    slot = place(hi, yy, core)

    def remote(src, dst, ssem, rsem, dev):
        return pltpu.make_async_remote_copy(
            src_ref=src,
            dst_ref=dst,
            send_sem=ssem,
            recv_sem=rsem,
            device_id={"node": dev},
            device_id_type=pl.DeviceIdType.MESH,
        )

    barrier = pltpu.get_barrier_semaphore()
    partners = [core_peer, y_peer] + [z_peer(k) for k in range(1, hi_n)]
    for dev in partners:
        pl.semaphore_signal(
            barrier, inc=1, device_id={"node": dev}, device_id_type=pl.DeviceIdType.MESH
        )

    pairs = [
        (prefix_hbm, prefix),
        (query_hbm, query),
        (lens_hbm, lens),
        (new_kv_hbm, new_kv),
        (cache_hbm, cache),
        (residual_hbm, residual),
        (gain_hbm, gain),
        (ids_hbm, ids),
        (router_hbm, router_w),
        (wg_hbm, wg),
        (wu_hbm, wu),
        (wd_hbm, wd),
    ]
    loads = [pltpu.make_async_copy(a, b, fetch.at[i]) for i, (a, b) in enumerate(pairs)]
    for load in loads:
        load.start()

    half = n // 2
    line = core * half + yy * hi_n
    other = core * half + (1 - yy) * hi_n

    class Gather:
        def __init__(self, buf, zs, zr, ys, yr, cs, cr):
            self.buf = buf
            self.cuts = buf.shape[0]
            self.sems = (zs, zr, ys, yr, cs, cr)
            self.sent = []

        def go(self, src, ssem, rsem, dev):
            copy = remote(src, src, ssem, rsem, dev)
            copy.start()
            self.sent.append(copy)

        def arrive(self, ref, sem):
            pltpu.make_async_copy(ref, ref, sem).wait()

        def first(self, c):
            zs, zr = self.sems[:2]
            for k in range(1, hi_n):
                self.go(self.buf.at[c, slot], zs.at[c, k - 1], zr.at[c, k - 1], z_peer(k))

        def from_z(self, c):
            zs, zr, ys, yr, cs, cr = self.sems
            for k in range(1, hi_n):
                at = place(lax.rem(hi + hi_n - k, hi_n), yy, core)
                self.arrive(self.buf.at[c, at], zr.at[c, k - 1])
            mine = self.buf.at[c, pl.ds(line, hi_n)]
            self.go(mine, ys.at[c], yr.at[c], y_peer)
            self.go(mine, cs.at[c, 0], cr.at[c, 0], core_peer)

        def from_y(self, c):
            zs, zr, ys, yr, cs, cr = self.sems
            ref = self.buf.at[c, pl.ds(other, hi_n)]
            self.arrive(ref, yr.at[c])
            self.go(ref, cs.at[c, 1], cr.at[c, 1], core_peer)

        def from_core(self, c):
            cr = self.sems[5]
            for side, y in ((0, yy), (1, 1 - yy)):
                ref = self.buf.at[c, pl.ds((1 - core) * half + y * hi_n, hi_n)]
                self.arrive(ref, cr.at[c, side])

        def drain(self):
            for copy in self.sent:
                copy.wait_send()

        def run(self, use, begun=0):
            for c in range(begun, self.cuts):
                self.from_z(c)
            self.from_y(0)
            for c in range(self.cuts):
                if c + 1 < self.cuts:
                    self.from_y(c + 1)
                self.from_core(c)
                use(c)

    loads[0].wait()
    span = KV_HEADS // PCUTS * HEAD
    for c in range(PCUTS):
        for kv in range(2):
            pbuf[c, slot, kv] = prefix[:, kv, c * span : (c + 1) * span]
    pl.semaphore_wait(barrier, len(partners))
    pre = Gather(pbuf, pzs, pzr, pys, pyr, pcs, pcr)
    for c in range(PCUTS):
        pre.first(c)

    for at in range(1, 4):
        loads[at].wait()
    nkv = new_kv[...].astype(F32)
    new_key = nkv[:, 0, :]
    new_val = nkv[:, 1, :]
    q32[...] = query[...].astype(F32)

    eye = iota((seqs, seqs), 0) == iota((seqs, seqs), 1)

    def column(row):
        return jnp.sum(jnp.where(eye, jnp.broadcast_to(row, (seqs, seqs)), 0.0), axis=1, keepdims=True)

    len_col = column(lens[...].astype(F32))
    live = iota((seqs, CACHE), 1).astype(F32) < len_col
    live = jnp.concatenate([live.astype(F32)] * GROUP, axis=0) > 0.0
    srow = lax.rem(iota((rows, CACHE), 0), seqs)
    loads[4].wait()

    def queries(g):
        return jnp.concatenate(
            [q32[:, (g * GROUP + r) * HEAD : (g * GROUP + r + 1) * HEAD] for r in range(GROUP)], axis=0
        )

    for g in range(KV_HEADS):
        lanes = slice(g * HEAD, (g + 1) * HEAD)
        q = queries(g)
        qb = q.astype(BF16)
        s = jnp.zeros((rows, CACHE), F32)
        for t in range(seqs):
            s = jnp.where(srow == t, mm(qb, cache[t, 0, :, lanes], NT), s)
        s = jnp.where(live, s * factor, NEG)
        nk = jnp.concatenate([new_key[:, lanes]] * GROUP, axis=0)
        own = jnp.sum(q * nk, axis=1, keepdims=True) * factor
        top = jnp.maximum(jnp.max(s, axis=1, keepdims=True), own)
        e = jnp.where(live, jnp.exp(s - top), 0.0)
        e_own = jnp.exp(own - top)
        den = jnp.sum(e, axis=1, keepdims=True) + e_own
        nv = jnp.concatenate([new_val[:, lanes]] * GROUP, axis=0)
        acc = e_own.astype(BF16).astype(F32) * nv
        for t in range(seqs):
            acc = acc + mm(jnp.where(srow == t, e, 0.0).astype(BF16), cache[t, 1, :, lanes])
        acc_ref[g] = acc
        top_ref[g] = jnp.broadcast_to(top, (rows, HEAD))
        den_ref[g] = jnp.broadcast_to(den, (rows, HEAD))
        if g == 5:
            pre.from_z(0)
        if g == 7:
            pre.from_z(1)

    for at in range(5, 9):
        loads[at].wait()

    count = n * prefix.shape[0]
    square = [jnp.zeros((seqs, HEAD), F32)]

    def attend(c):
        for part in range(KV_HEADS // PCUTS):
            g = c * (KV_HEADS // PCUTS) + part
            lanes = slice(part * HEAD, (part + 1) * HEAD)
            qb = queries(g).astype(BF16)
            keys = pbuf[c, :, 0, :, lanes].reshape(count, HEAD)
            vals = pbuf[c, :, 1, :, lanes].reshape(count, HEAD)
            s = mm(qb, keys, NT) * factor
            best = top_ref[g][:, :1]
            top = jnp.maximum(best, jnp.max(s, axis=1, keepdims=True))
            shrink = jnp.exp(best - top)
            e = jnp.exp(s - top)
            den = den_ref[g][:, :1] * shrink + jnp.sum(e, axis=1, keepdims=True)
            acc = acc_ref[g] * shrink + mm(e.astype(BF16), vals)
            attn = (acc / den).astype(BF16).astype(F32)
            for r in range(GROUP):
                at = slice((g * GROUP + r) * HEAD, (g * GROUP + r + 1) * HEAD)
                h = residual[:, at].astype(F32) + attn[r * seqs : (r + 1) * seqs]
                hidden_ref[:, at] = h
                square[0] = square[0] + h * h

    pre.run(attend, 2)
    square = square[0]

    scale = lax.rsqrt(jnp.sum(square, axis=1, keepdims=True) / d + 1e-5)
    normed = (hidden_ref[...] * scale * gain[...]).astype(BF16)

    routed_row = jnp.zeros((1, seqs), F32)
    for j in range(TOP):
        routed_row = jnp.maximum(routed_row, (ids[j : j + 1, :] == 0).astype(F32))
    routed_col = column(routed_row)
    before = jnp.where(iota((seqs, seqs), 0) < iota((seqs, seqs), 1), routed_col, 0.0)
    rank_row = jnp.sum(before, axis=0, keepdims=True)
    picks = []
    for p in range(PIECES):
        at = (iota((CAP * PIECES, seqs), 0) - CAP * p).astype(F32)
        picks.append(jnp.where((at == rank_row) & (routed_row > 0.0), 1.0, 0.0).astype(BF16))
    tok = Gather(xbuf, xzs, xzr, xys, xyr, xcs, xcr)
    for c in range(CUTS):
        packed = jnp.zeros((CAP * PIECES, thin), F32)
        for p in range(PIECES):
            lo = c * wide + p * thin
            packed = packed + mm(picks[p], normed[:, lo : lo + thin])
        xbuf[c, slot] = packed.astype(BF16)
        tok.first(c)

    logits = mm(normed, router_w[...], NT)
    expo = jnp.exp(logits - jnp.max(logits, axis=1, keepdims=True))
    router = expo / jnp.sum(expo, axis=1, keepdims=True)
    expert = iota((seqs, EXPERTS), 1).astype(F32)
    chosen = jnp.zeros((seqs, EXPERTS), F32)
    for j in range(TOP):
        chosen = chosen + (expert == column(ids[j : j + 1, :].astype(F32))).astype(F32)
    picked = jnp.sum(router * chosen, axis=1, keepdims=True)
    weight = jnp.where(routed_col > 0.0, router[:, :1], 0.0) / picked
    rank_col = column(rank_row)

    size = CAP * n
    across = CAP * PIECES * n
    a = iota((across, across), 0)
    b = iota((across, across), 1)
    def packed_row(x):
        return CAP * PIECES * (lax.rem(x, size) // CAP) + CAP * (x // size) + lax.rem(x, CAP)

    to_stack = (packed_row(a) == b).astype(F32).astype(BF16)
    to_pack = (packed_row(b) == a).astype(F32).astype(BF16)

    loads[9].wait()
    loads[10].wait()

    def gate_up(c):
        stacked = mm(to_stack, xbuf[c].reshape(across, thin)).astype(BF16)
        x = jnp.concatenate([stacked[p * size : (p + 1) * size] for p in range(PIECES)], axis=1)
        gate = mm(x, wg[:, c * wide : (c + 1) * wide], NT)
        upper = mm(x, wu[:, c * wide : (c + 1) * wide], NT)
        if c:
            gate = gate + gate_ref[...]
            upper = upper + upper_ref[...]
        if c < CUTS - 1:
            gate_ref[...] = gate
            upper_ref[...] = upper
        else:
            inner_ref[...] = (gate / (1.0 + jnp.exp(-gate)) * upper).astype(BF16)

    tok.run(gate_up)

    loads[11].wait()

    def hop1(c):
        src = msg.at[c, pl.ds((1 - core) * half, half)]
        return remote(src, got_core.at[c], csend.at[c], crecv.at[c], core_peer)

    def hop2(c):
        src = sum_core.at[c, pl.ds((1 - yy) * hi_n, hi_n)]
        return remote(src, got_y.at[c], ysend.at[c], yrecv.at[c], y_peer)

    def hop3(c, k):
        h = lax.rem(hi + k, hi_n)
        return remote(
            sum_y.at[c, h], got_z.at[c, k - 1], zsend.at[c, k - 1], zrecv.at[c, k - 1], z_peer(k)
        )

    def work(c):
        y = mm(inner_ref[...], wd[:, c * wide : (c + 1) * wide]).astype(BF16)
        for piece in range(PIECES):
            ystack[c, piece * size : (piece + 1) * size, :] = y[:, piece * thin : (piece + 1) * thin]
        full = mm(to_pack, ystack[c]).astype(BF16)
        msg[c] = full.reshape(n, CAP * PIECES, thin)
        hop1(c).start()

    def add_core(c):
        hop1(c).wait_recv()
        total = msg[c, pl.ds(core * half, half)].astype(F32) + got_core[c].astype(F32)
        sum_core[c] = total.astype(BF16)
        hop2(c).start()

    def add_y(c):
        hop2(c).wait_recv()
        total = sum_core[c, pl.ds(yy * hi_n, hi_n)].astype(F32) + got_y[c].astype(F32)
        sum_y[c] = total.astype(BF16)
        for k in range(1, hi_n):
            hop3(c, k).start()

    def finish(c):
        total = sum_y[c, hi].astype(F32)
        for k in range(1, hi_n):
            hop3(c, k).wait_recv()
            total = total + got_z[c, k - 1].astype(F32)
        for piece in range(PIECES):
            lo = c * wide + piece * thin
            y = jnp.zeros((seqs, thin), F32)
            for k in range(CAP):
                mine = (rank_col == float(k)) & (routed_col > 0.0)
                at = piece * CAP + k
                y = y + jnp.where(mine, total[at : at + 1, :], 0.0)
            out[:, lo : lo + thin] = (hidden_ref[:, lo : lo + thin] + weight * y).astype(BF16)

    work(0)
    for c in range(1, CUTS):
        work(c)
        add_core(c - 1)
    add_core(CUTS - 1)
    for c in range(CUTS):
        add_y(c)
    for c in range(CUTS):
        finish(c)

    pre.drain()
    tok.drain()
    for c in range(CUTS):
        hop1(c).wait_send()
        hop2(c).wait_send()
        for k in range(1, hi_n):
            hop3(c, k).wait_send()


def body(n, query, new_kv, cache_kv, cache_len, prefix_kv, residual_in, norm_gain, router_w, expert_ids, w_gate, w_up, w_down):
    seqs, d = query.shape
    ff = w_down.shape[0]
    per = prefix_kv.shape[0]
    width = KV_HEADS * HEAD
    rows = seqs * GROUP
    wide = d // CUTS
    thin = wide // PIECES
    packs = CAP * PIECES
    hi_n = n // 4
    hops = max(hi_n - 1, 1)
    vmem = pl.BlockSpec(memory_space=pltpu.VMEM)
    hbm = pl.BlockSpec(memory_space=pl.ANY)
    dma = pltpu.SemaphoreType.DMA
    return pl.pallas_call(
        functools.partial(kernel, n),
        out_shape=jax.ShapeDtypeStruct((seqs, d), BF16),
        in_specs=[hbm] * 12,
        out_specs=vmem,
        scratch_shapes=[
            pltpu.VMEM((seqs, d), BF16),
            pltpu.VMEM((seqs, 2, width), BF16),
            pltpu.VMEM((seqs, 2, CACHE, width), BF16),
            pltpu.VMEM((1, seqs), jnp.int32),
            pltpu.VMEM((per, 2, width), BF16),
            pltpu.VMEM((seqs, d), BF16),
            pltpu.VMEM((1, d), F32),
            pltpu.VMEM((EXPERTS, d), BF16),
            pltpu.VMEM((TOP, seqs), jnp.int32),
            pltpu.VMEM((ff, d), BF16),
            pltpu.VMEM((ff, d), BF16),
            pltpu.VMEM((ff, d), BF16),
            pltpu.VMEM((PCUTS, n, 2, per, width // PCUTS), BF16),
            pltpu.VMEM((seqs, d), F32),
            pltpu.VMEM((KV_HEADS, rows, HEAD), F32),
            pltpu.VMEM((KV_HEADS, rows, HEAD), F32),
            pltpu.VMEM((KV_HEADS, rows, HEAD), F32),
            pltpu.VMEM((seqs, d), F32),
            pltpu.VMEM((CUTS, n, packs, thin), BF16),
            pltpu.VMEM((CAP * n, ff), F32),
            pltpu.VMEM((CAP * n, ff), F32),
            pltpu.VMEM((CAP * n, ff), BF16),
            pltpu.VMEM((CUTS, n * packs, thin), BF16),
            pltpu.VMEM((CUTS, n, packs, thin), BF16),
            pltpu.VMEM((CUTS, n // 2, packs, thin), BF16),
            pltpu.VMEM((CUTS, n // 2, packs, thin), BF16),
            pltpu.VMEM((CUTS, hi_n, packs, thin), BF16),
            pltpu.VMEM((CUTS, hi_n, packs, thin), BF16),
            pltpu.VMEM((CUTS, hops, packs, thin), BF16),
            dma((12,)),
            dma((PCUTS, hops)),
            dma((PCUTS, hops)),
            dma((PCUTS,)),
            dma((PCUTS,)),
            dma((PCUTS, 2)),
            dma((PCUTS, 2)),
            dma((CUTS, hops)),
            dma((CUTS, hops)),
            dma((CUTS,)),
            dma((CUTS,)),
            dma((CUTS, 2)),
            dma((CUTS, 2)),
            dma((CUTS,)),
            dma((CUTS,)),
            dma((CUTS,)),
            dma((CUTS,)),
            dma((CUTS, hops)),
            dma((CUTS, hops)),
        ],
        compiler_params=pltpu.CompilerParams(
            collective_id=0, has_side_effects=True, vmem_limit_bytes=60 * 1024 * 1024
        ),
        cost_estimate=pl.CostEstimate(
            flops=6 * CAP * n * d * ff, bytes_accessed=6 * d * ff + 2 * cache_kv.size, transcendentals=0
        ),
    )(
        query,
        new_kv,
        cache_kv,
        cache_len.reshape(1, seqs),
        prefix_kv,
        residual_in,
        norm_gain.reshape(1, d),
        router_w.T,
        expert_ids.T,
        w_gate.T,
        w_up.T,
        w_down,
    )


def solution(mesh):
    return jax.shard_map(
        functools.partial(body, mesh.shape["node"]),
        mesh=mesh,
        in_specs=(
            P(("groups", "node"), None),
            P(("groups", "node"), None, None),
            P(("groups", "node"), None, None, None),
            P(("groups", "node")),
            P(("groups", "node"), None, None),
            P(("groups", "node"), None),
            P(),
            P(),
            P(("groups", "node"), None),
            P(None, "node"),
            P(None, "node"),
            P("node", None),
        ),
        out_specs=P(("groups", "node"), None),
        check_vma=False,
    )
```

```python
import functools

import jax
import jax.numpy as jnp
from jax import lax
from jax.experimental import pallas as pl
from jax.experimental.pallas import tpu as pltpu
from jax.sharding import PartitionSpec as P

HEADS = 48
KV_HEADS = 8
GROUP = HEADS // KV_HEADS
HEAD = 128
EXPERTS = 16
TOP = 4
CACHE = 128
CAP = 4
PCUTS = 4
CUTS = 4
PIECES = 4
NEG = -1e30
F32 = jnp.float32
BF16 = jnp.bfloat16
NT = (((1,), (1,)), ((), ()))
NN = (((1,), (0,)), ((), ()))


def mm(a, b, dims=NN):
    return lax.dot_general(a, b, dims, preferred_element_type=F32)


def iota(shape, dim):
    return lax.broadcasted_iota(jnp.int32, shape, dim)


def kernel(
    n,
    query_hbm,
    new_kv_hbm,
    cache_hbm,
    lens_hbm,
    prefix_hbm,
    residual_hbm,
    gain_hbm,
    router_hbm,
    ids_hbm,
    wg_hbm,
    wu_hbm,
    wd_hbm,
    out,
    query,
    new_kv,
    cache,
    lens,
    prefix,
    residual,
    gain,
    router_w,
    ids,
    wg,
    wu,
    wd,
    pbuf,
    q32,
    acc_ref,
    top_ref,
    den_ref,
    hidden_ref,
    xbuf,
    perms,
    gate_ref,
    upper_ref,
    inner_ref,
    ystack,
    msg,
    got_core,
    sum_core,
    got_y,
    sum_y,
    got_z,
    fetch,
    pzs,
    pzr,
    pys,
    pyr,
    pcs,
    pcr,
    xzs,
    xzr,
    xys,
    xyr,
    xcs,
    xcr,
    csend,
    crecv,
    ysend,
    yrecv,
    zsend,
    zrecv,
):
    seqs, d = query.shape
    ff = wg.shape[0]
    hi_n = n // 4
    rows = seqs * GROUP
    wide = d // CUTS
    thin = wide // PIECES
    factor = HEAD ** (-0.5)
    me = lax.axis_index("node")
    core = lax.rem(me, 2)
    yy = lax.rem(me // 2, 2)
    hi = me // 4
    core_peer = hi * 4 + yy * 2 + (1 - core)
    y_peer = hi * 4 + (1 - yy) * 2 + core

    def z_peer(k):
        return lax.rem(hi + k, hi_n) * 4 + yy * 2 + core

    def place(h, y, c):
        return c * (n // 2) + y * hi_n + h

    slot = place(hi, yy, core)

    def remote(src, dst, ssem, rsem, dev):
        return pltpu.make_async_remote_copy(
            src_ref=src,
            dst_ref=dst,
            send_sem=ssem,
            recv_sem=rsem,
            device_id={"node": dev},
            device_id_type=pl.DeviceIdType.MESH,
        )

    barrier = pltpu.get_barrier_semaphore()
    partners = [core_peer, y_peer] + [z_peer(k) for k in range(1, hi_n)]
    for dev in partners:
        pl.semaphore_signal(
            barrier, inc=1, device_id={"node": dev}, device_id_type=pl.DeviceIdType.MESH
        )

    pairs = [
        (prefix_hbm, prefix),
        (query_hbm, query),
        (lens_hbm, lens),
        (new_kv_hbm, new_kv),
        (cache_hbm, cache),
        (residual_hbm, residual),
        (gain_hbm, gain),
        (ids_hbm, ids),
        (router_hbm, router_w),
        (wg_hbm, wg),
        (wu_hbm, wu),
        (wd_hbm, wd),
    ]
    loads = [pltpu.make_async_copy(a, b, fetch.at[i]) for i, (a, b) in enumerate(pairs)]
    for load in loads:
        load.start()

    half = n // 2
    line = core * half + yy * hi_n
    other = core * half + (1 - yy) * hi_n

    class Gather:
        def __init__(self, buf, zs, zr, ys, yr, cs, cr):
            self.buf = buf
            self.cuts = buf.shape[0]
            self.sems = (zs, zr, ys, yr, cs, cr)
            self.sent = []

        def go(self, src, ssem, rsem, dev):
            copy = remote(src, src, ssem, rsem, dev)
            copy.start()
            self.sent.append(copy)

        def arrive(self, ref, sem):
            pltpu.make_async_copy(ref, ref, sem).wait()

        def first(self, c):
            zs, zr = self.sems[:2]
            for k in range(1, hi_n):
                self.go(self.buf.at[c, slot], zs.at[c, k - 1], zr.at[c, k - 1], z_peer(k))

        def from_z(self, c):
            zs, zr, ys, yr, cs, cr = self.sems
            for k in range(1, hi_n):
                at = place(lax.rem(hi + hi_n - k, hi_n), yy, core)
                self.arrive(self.buf.at[c, at], zr.at[c, k - 1])
            mine = self.buf.at[c, pl.ds(line, hi_n)]
            self.go(mine, ys.at[c], yr.at[c], y_peer)
            self.go(mine, cs.at[c, 0], cr.at[c, 0], core_peer)

        def from_y(self, c):
            zs, zr, ys, yr, cs, cr = self.sems
            ref = self.buf.at[c, pl.ds(other, hi_n)]
            self.arrive(ref, yr.at[c])
            self.go(ref, cs.at[c, 1], cr.at[c, 1], core_peer)

        def from_core(self, c):
            cr = self.sems[5]
            for side, y in ((0, yy), (1, 1 - yy)):
                ref = self.buf.at[c, pl.ds((1 - core) * half + y * hi_n, hi_n)]
                self.arrive(ref, cr.at[c, side])

        def drain(self):
            for copy in self.sent:
                copy.wait_send()

        def run(self, use, begun=0):
            for c in range(begun, self.cuts):
                self.from_z(c)
            self.from_y(0)
            for c in range(self.cuts):
                if c + 1 < self.cuts:
                    self.from_y(c + 1)
                self.from_core(c)
                use(c)

    loads[0].wait()
    span = KV_HEADS // PCUTS * HEAD
    for c in range(PCUTS):
        for kv in range(2):
            pbuf[c, slot, kv] = prefix[:, kv, c * span : (c + 1) * span]
    pl.semaphore_wait(barrier, len(partners))
    pre = Gather(pbuf, pzs, pzr, pys, pyr, pcs, pcr)
    for c in range(PCUTS):
        pre.first(c)

    for at in range(1, 4):
        loads[at].wait()
    nkv = new_kv[...].astype(F32)
    new_key = nkv[:, 0, :]
    new_val = nkv[:, 1, :]
    q32[...] = query[...].astype(F32)

    eye = iota((seqs, seqs), 0) == iota((seqs, seqs), 1)

    def column(row):
        return jnp.sum(jnp.where(eye, jnp.broadcast_to(row, (seqs, seqs)), 0.0), axis=1, keepdims=True)

    len_col = column(lens[...].astype(F32))
    live = iota((seqs, CACHE), 1).astype(F32) < len_col
    live = jnp.concatenate([live.astype(F32)] * GROUP, axis=0) > 0.0
    srow = lax.rem(iota((rows, CACHE), 0), seqs)
    loads[4].wait()

    def queries(g):
        return jnp.concatenate(
            [q32[:, (g * GROUP + r) * HEAD : (g * GROUP + r + 1) * HEAD] for r in range(GROUP)], axis=0
        )

    for g in range(KV_HEADS):
        lanes = slice(g * HEAD, (g + 1) * HEAD)
        q = queries(g)
        qb = q.astype(BF16)
        s = jnp.zeros((rows, CACHE), F32)
        for t in range(seqs):
            s = jnp.where(srow == t, mm(qb, cache[t, 0, :, lanes], NT), s)
        s = jnp.where(live, s * factor, NEG)
        nk = jnp.concatenate([new_key[:, lanes]] * GROUP, axis=0)
        own = jnp.sum(q * nk, axis=1, keepdims=True) * factor
        top = jnp.maximum(jnp.max(s, axis=1, keepdims=True), own)
        e = jnp.where(live, jnp.exp(s - top), 0.0)
        e_own = jnp.exp(own - top)
        den = jnp.sum(e, axis=1, keepdims=True) + e_own
        nv = jnp.concatenate([new_val[:, lanes]] * GROUP, axis=0)
        acc = e_own.astype(BF16).astype(F32) * nv
        for t in range(seqs):
            acc = acc + mm(jnp.where(srow == t, e, 0.0).astype(BF16), cache[t, 1, :, lanes])
        acc_ref[g] = acc
        top_ref[g] = jnp.broadcast_to(top, (rows, HEAD))
        den_ref[g] = jnp.broadcast_to(den, (rows, HEAD))
        if g == 5:
            pre.from_z(0)
        if g == 7:
            pre.from_z(1)

    size = CAP * n
    across = CAP * PIECES * n

    def packed_row(x):
        return CAP * PIECES * (lax.rem(x, size) // CAP) + CAP * (x // size) + lax.rem(x, CAP)

    square_at = (across, across)
    perms[0] = (packed_row(iota((across, 1), 0)) == iota(square_at, 1)).astype(F32).astype(BF16)
    perms[1] = (packed_row(iota((1, across), 1)) == iota(square_at, 0)).astype(F32).astype(BF16)

    for at in range(5, 9):
        loads[at].wait()

    count = n * prefix.shape[0]
    square = [jnp.zeros((seqs, HEAD), F32)]

    def attend(c):
        for part in range(KV_HEADS // PCUTS):
            g = c * (KV_HEADS // PCUTS) + part
            lanes = slice(part * HEAD, (part + 1) * HEAD)
            qb = queries(g).astype(BF16)
            keys = pbuf[c, :, 0, :, lanes].reshape(count, HEAD)
            vals = pbuf[c, :, 1, :, lanes].reshape(count, HEAD)
            s = mm(qb, keys, NT) * factor
            best = top_ref[g][:, :1]
            top = jnp.maximum(best, jnp.max(s, axis=1, keepdims=True))
            shrink = jnp.exp(best - top)
            e = jnp.exp(s - top)
            den = den_ref[g][:, :1] * shrink + jnp.sum(e, axis=1, keepdims=True)
            acc = acc_ref[g] * shrink + mm(e.astype(BF16), vals)
            attn = (acc / den).astype(BF16).astype(F32)
            for r in range(GROUP):
                at = slice((g * GROUP + r) * HEAD, (g * GROUP + r + 1) * HEAD)
                h = residual[:, at].astype(F32) + attn[r * seqs : (r + 1) * seqs]
                hidden_ref[:, at] = h
                square[0] = square[0] + h * h

    pre.run(attend, 2)
    square = square[0]

    scale = lax.rsqrt(jnp.sum(square, axis=1, keepdims=True) / d + 1e-5)
    normed = (hidden_ref[...] * scale * gain[...]).astype(BF16)

    routed_row = jnp.zeros((1, seqs), F32)
    for j in range(TOP):
        routed_row = jnp.maximum(routed_row, (ids[j : j + 1, :] == 0).astype(F32))
    routed_col = column(routed_row)
    before = jnp.where(iota((seqs, seqs), 0) < iota((seqs, seqs), 1), routed_col, 0.0)
    rank_row = jnp.sum(before, axis=0, keepdims=True)
    picks = []
    for p in range(PIECES):
        at = (iota((CAP * PIECES, seqs), 0) - CAP * p).astype(F32)
        picks.append(jnp.where((at == rank_row) & (routed_row > 0.0), 1.0, 0.0).astype(BF16))
    tok = Gather(xbuf, xzs, xzr, xys, xyr, xcs, xcr)
    for c in range(CUTS):
        packed = jnp.zeros((CAP * PIECES, thin), F32)
        for p in range(PIECES):
            lo = c * wide + p * thin
            packed = packed + mm(picks[p], normed[:, lo : lo + thin])
        xbuf[c, slot] = packed.astype(BF16)
        tok.first(c)

    logits = mm(normed, router_w[...], NT)
    expo = jnp.exp(logits - jnp.max(logits, axis=1, keepdims=True))
    router = expo / jnp.sum(expo, axis=1, keepdims=True)
    expert = iota((seqs, EXPERTS), 1).astype(F32)
    chosen = jnp.zeros((seqs, EXPERTS), F32)
    for j in range(TOP):
        chosen = chosen + (expert == column(ids[j : j + 1, :].astype(F32))).astype(F32)
    picked = jnp.sum(router * chosen, axis=1, keepdims=True)
    weight = jnp.where(routed_col > 0.0, router[:, :1], 0.0) / picked
    rank_col = column(rank_row)

    loads[9].wait()
    loads[10].wait()

    def gate_up(c):
        stacked = mm(perms[0], xbuf[c].reshape(across, thin)).astype(BF16)
        x = jnp.concatenate([stacked[p * size : (p + 1) * size] for p in range(PIECES)], axis=1)
        gate = mm(x, wg[:, c * wide : (c + 1) * wide], NT)
        upper = mm(x, wu[:, c * wide : (c + 1) * wide], NT)
        if c:
            gate = gate + gate_ref[...]
            upper = upper + upper_ref[...]
        if c < CUTS - 1:
            gate_ref[...] = gate
            upper_ref[...] = upper
        else:
            inner_ref[...] = (gate / (1.0 + jnp.exp(-gate)) * upper).astype(BF16)

    tok.run(gate_up)

    loads[11].wait()

    def hop1(c):
        src = msg.at[c, pl.ds((1 - core) * half, half)]
        return remote(src, got_core.at[c], csend.at[c], crecv.at[c], core_peer)

    def hop2(c):
        src = sum_core.at[c, pl.ds((1 - yy) * hi_n, hi_n)]
        return remote(src, got_y.at[c], ysend.at[c], yrecv.at[c], y_peer)

    def hop3(c, k):
        h = lax.rem(hi + k, hi_n)
        return remote(
            sum_y.at[c, h], got_z.at[c, k - 1], zsend.at[c, k - 1], zrecv.at[c, k - 1], z_peer(k)
        )

    def work(c):
        y = mm(inner_ref[...], wd[:, c * wide : (c + 1) * wide]).astype(BF16)
        for piece in range(PIECES):
            ystack[c, piece * size : (piece + 1) * size, :] = y[:, piece * thin : (piece + 1) * thin]
        full = mm(perms[1], ystack[c]).astype(BF16)
        msg[c] = full.reshape(n, CAP * PIECES, thin)
        hop1(c).start()

    def add_core(c):
        hop1(c).wait_recv()
        total = msg[c, pl.ds(core * half, half)].astype(F32) + got_core[c].astype(F32)
        sum_core[c] = total.astype(BF16)
        hop2(c).start()

    def add_y(c):
        hop2(c).wait_recv()
        total = sum_core[c, pl.ds(yy * hi_n, hi_n)].astype(F32) + got_y[c].astype(F32)
        sum_y[c] = total.astype(BF16)
        for k in range(1, hi_n):
            hop3(c, k).start()

    def finish(c):
        total = sum_y[c, hi].astype(F32)
        for k in range(1, hi_n):
            hop3(c, k).wait_recv()
            total = total + got_z[c, k - 1].astype(F32)
        for piece in range(PIECES):
            lo = c * wide + piece * thin
            y = jnp.zeros((seqs, thin), F32)
            for k in range(CAP):
                mine = (rank_col == float(k)) & (routed_col > 0.0)
                at = piece * CAP + k
                y = y + jnp.where(mine, total[at : at + 1, :], 0.0)
            out[:, lo : lo + thin] = (hidden_ref[:, lo : lo + thin] + weight * y).astype(BF16)

    work(0)
    for c in range(1, CUTS):
        work(c)
        add_core(c - 1)
    add_core(CUTS - 1)
    for c in range(CUTS):
        add_y(c)
    for c in range(CUTS):
        finish(c)

    pre.drain()
    tok.drain()
    for c in range(CUTS):
        hop1(c).wait_send()
        hop2(c).wait_send()
        for k in range(1, hi_n):
            hop3(c, k).wait_send()


def body(n, query, new_kv, cache_kv, cache_len, prefix_kv, residual_in, norm_gain, router_w, expert_ids, w_gate, w_up, w_down):
    seqs, d = query.shape
    ff = w_down.shape[0]
    per = prefix_kv.shape[0]
    width = KV_HEADS * HEAD
    rows = seqs * GROUP
    wide = d // CUTS
    thin = wide // PIECES
    packs = CAP * PIECES
    hi_n = n // 4
    hops = max(hi_n - 1, 1)
    vmem = pl.BlockSpec(memory_space=pltpu.VMEM)
    hbm = pl.BlockSpec(memory_space=pl.ANY)
    dma = pltpu.SemaphoreType.DMA
    return pl.pallas_call(
        functools.partial(kernel, n),
        out_shape=jax.ShapeDtypeStruct((seqs, d), BF16),
        in_specs=[hbm] * 12,
        out_specs=vmem,
        scratch_shapes=[
            pltpu.VMEM((seqs, d), BF16),
            pltpu.VMEM((seqs, 2, width), BF16),
            pltpu.VMEM((seqs, 2, CACHE, width), BF16),
            pltpu.VMEM((1, seqs), jnp.int32),
            pltpu.VMEM((per, 2, width), BF16),
            pltpu.VMEM((seqs, d), BF16),
            pltpu.VMEM((1, d), F32),
            pltpu.VMEM((EXPERTS, d), BF16),
            pltpu.VMEM((TOP, seqs), jnp.int32),
            pltpu.VMEM((ff, d), BF16),
            pltpu.VMEM((ff, d), BF16),
            pltpu.VMEM((ff, d), BF16),
            pltpu.VMEM((PCUTS, n, 2, per, width // PCUTS), BF16),
            pltpu.VMEM((seqs, d), F32),
            pltpu.VMEM((KV_HEADS, rows, HEAD), F32),
            pltpu.VMEM((KV_HEADS, rows, HEAD), F32),
            pltpu.VMEM((KV_HEADS, rows, HEAD), F32),
            pltpu.VMEM((seqs, d), F32),
            pltpu.VMEM((CUTS, n, packs, thin), BF16),
            pltpu.VMEM((2, n * packs, n * packs), BF16),
            pltpu.VMEM((CAP * n, ff), F32),
            pltpu.VMEM((CAP * n, ff), F32),
            pltpu.VMEM((CAP * n, ff), BF16),
            pltpu.VMEM((CUTS, n * packs, thin), BF16),
            pltpu.VMEM((CUTS, n, packs, thin), BF16),
            pltpu.VMEM((CUTS, n // 2, packs, thin), BF16),
            pltpu.VMEM((CUTS, n // 2, packs, thin), BF16),
            pltpu.VMEM((CUTS, hi_n, packs, thin), BF16),
            pltpu.VMEM((CUTS, hi_n, packs, thin), BF16),
            pltpu.VMEM((CUTS, hops, packs, thin), BF16),
            dma((12,)),
            dma((PCUTS, hops)),
            dma((PCUTS, hops)),
            dma((PCUTS,)),
            dma((PCUTS,)),
            dma((PCUTS, 2)),
            dma((PCUTS, 2)),
            dma((CUTS, hops)),
            dma((CUTS, hops)),
            dma((CUTS,)),
            dma((CUTS,)),
            dma((CUTS, 2)),
            dma((CUTS, 2)),
            dma((CUTS,)),
            dma((CUTS,)),
            dma((CUTS,)),
            dma((CUTS,)),
            dma((CUTS, hops)),
            dma((CUTS, hops)),
        ],
        compiler_params=pltpu.CompilerParams(
            collective_id=0, has_side_effects=True, vmem_limit_bytes=60 * 1024 * 1024
        ),
        cost_estimate=pl.CostEstimate(
            flops=6 * CAP * n * d * ff, bytes_accessed=6 * d * ff + 2 * cache_kv.size, transcendentals=0
        ),
    )(
        query,
        new_kv,
        cache_kv,
        cache_len.reshape(1, seqs),
        prefix_kv,
        residual_in,
        norm_gain.reshape(1, d),
        router_w.T,
        expert_ids.T,
        w_gate.T,
        w_up.T,
        w_down,
    )


def solution(mesh):
    return jax.shard_map(
        functools.partial(body, mesh.shape["node"]),
        mesh=mesh,
        in_specs=(
            P(("groups", "node"), None),
            P(("groups", "node"), None, None),
            P(("groups", "node"), None, None, None),
            P(("groups", "node")),
            P(("groups", "node"), None, None),
            P(("groups", "node"), None),
            P(),
            P(),
            P(("groups", "node"), None),
            P(None, "node"),
            P(None, "node"),
            P("node", None),
        ),
        out_specs=P(("groups", "node"), None),
        check_vma=False,
    )
```

```python
import functools

import jax
import jax.numpy as jnp
from jax import lax
from jax.experimental import pallas as pl
from jax.experimental.pallas import tpu as pltpu
from jax.sharding import PartitionSpec as P

HEADS = 48
KV_HEADS = 8
GROUP = HEADS // KV_HEADS
HEAD = 128
EXPERTS = 16
TOP = 4
CACHE = 128
CAP = 4
PCUTS = 4
CUTS = 4
PIECES = 4
NEG = -1e30
F32 = jnp.float32
BF16 = jnp.bfloat16
NT = (((1,), (1,)), ((), ()))
NN = (((1,), (0,)), ((), ()))


def mm(a, b, dims=NN):
    return lax.dot_general(a, b, dims, preferred_element_type=F32)


def iota(shape, dim):
    return lax.broadcasted_iota(jnp.int32, shape, dim)


def kernel(
    n,
    query_hbm,
    new_kv_hbm,
    cache_hbm,
    lens_hbm,
    prefix_hbm,
    residual_hbm,
    gain_hbm,
    router_hbm,
    ids_hbm,
    wg_hbm,
    wu_hbm,
    wd_hbm,
    out,
    query,
    new_kv,
    cache,
    lens,
    prefix,
    residual,
    gain,
    router_w,
    ids,
    wg,
    wu,
    wd,
    pbuf,
    q32,
    acc_ref,
    top_ref,
    den_ref,
    hidden_ref,
    xbuf,
    perms,
    gate_ref,
    upper_ref,
    inner_ref,
    ystack,
    msg,
    got_core,
    sum_core,
    got_y,
    sum_y,
    got_z,
    fetch,
    pzs,
    pzr,
    pys,
    pyr,
    pcs,
    pcr,
    xzs,
    xzr,
    xys,
    xyr,
    xcs,
    xcr,
    csend,
    crecv,
    ysend,
    yrecv,
    zsend,
    zrecv,
):
    seqs, d = query.shape
    ff = wg.shape[0]
    hi_n = n // 4
    rows = seqs * GROUP
    wide = d // CUTS
    thin = wide // PIECES
    factor = HEAD ** (-0.5)
    me = lax.axis_index("node")
    core = lax.rem(me, 2)
    yy = lax.rem(me // 2, 2)
    hi = me // 4
    core_peer = hi * 4 + yy * 2 + (1 - core)
    y_peer = hi * 4 + (1 - yy) * 2 + core

    def z_peer(k):
        return lax.rem(hi + k, hi_n) * 4 + yy * 2 + core

    def place(h, y, c):
        return c * (n // 2) + y * hi_n + h

    slot = place(hi, yy, core)

    def remote(src, dst, ssem, rsem, dev):
        return pltpu.make_async_remote_copy(
            src_ref=src,
            dst_ref=dst,
            send_sem=ssem,
            recv_sem=rsem,
            device_id={"node": dev},
            device_id_type=pl.DeviceIdType.MESH,
        )

    barrier = pltpu.get_barrier_semaphore()
    partners = [core_peer, y_peer] + [z_peer(k) for k in range(1, hi_n)]
    for dev in partners:
        pl.semaphore_signal(
            barrier, inc=1, device_id={"node": dev}, device_id_type=pl.DeviceIdType.MESH
        )

    pairs = [
        (prefix_hbm, prefix),
        (query_hbm, query),
        (lens_hbm, lens),
        (new_kv_hbm, new_kv),
        (cache_hbm, cache),
        (residual_hbm, residual),
        (gain_hbm, gain),
        (ids_hbm, ids),
        (router_hbm, router_w),
        (wg_hbm, wg),
        (wu_hbm, wu),
        (wd_hbm, wd),
    ]
    loads = [pltpu.make_async_copy(a, b, fetch.at[i]) for i, (a, b) in enumerate(pairs)]
    for load in loads:
        load.start()

    half = n // 2
    line = core * half + yy * hi_n
    other = core * half + (1 - yy) * hi_n

    class Gather:
        def __init__(self, buf, zs, zr, ys, yr, cs, cr):
            self.buf = buf
            self.cuts = buf.shape[0]
            self.sems = (zs, zr, ys, yr, cs, cr)
            self.sent = []

        def go(self, src, ssem, rsem, dev):
            copy = remote(src, src, ssem, rsem, dev)
            copy.start()
            self.sent.append(copy)

        def arrive(self, ref, sem):
            pltpu.make_async_copy(ref, ref, sem).wait()

        def first(self, c):
            zs, zr = self.sems[:2]
            for k in range(1, hi_n):
                self.go(self.buf.at[c, slot], zs.at[c, k - 1], zr.at[c, k - 1], z_peer(k))

        def from_z(self, c):
            zs, zr, ys, yr, cs, cr = self.sems
            for k in range(1, hi_n):
                at = place(lax.rem(hi + hi_n - k, hi_n), yy, core)
                self.arrive(self.buf.at[c, at], zr.at[c, k - 1])
            mine = self.buf.at[c, pl.ds(line, hi_n)]
            self.go(mine, ys.at[c], yr.at[c], y_peer)
            self.go(mine, cs.at[c, 0], cr.at[c, 0], core_peer)

        def from_y(self, c):
            zs, zr, ys, yr, cs, cr = self.sems
            ref = self.buf.at[c, pl.ds(other, hi_n)]
            self.arrive(ref, yr.at[c])
            self.go(ref, cs.at[c, 1], cr.at[c, 1], core_peer)

        def from_core(self, c):
            cr = self.sems[5]
            for side, y in ((0, yy), (1, 1 - yy)):
                ref = self.buf.at[c, pl.ds((1 - core) * half + y * hi_n, hi_n)]
                self.arrive(ref, cr.at[c, side])

        def drain(self):
            for copy in self.sent:
                copy.wait_send()

        def run(self, use, begun=0):
            for c in range(begun, self.cuts):
                self.from_z(c)
            self.from_y(0)
            for c in range(self.cuts):
                if c + 1 < self.cuts:
                    self.from_y(c + 1)
                self.from_core(c)
                use(c)

    loads[0].wait()
    span = KV_HEADS // PCUTS * HEAD
    for c in range(PCUTS):
        for kv in range(2):
            pbuf[c, slot, kv] = prefix[:, kv, c * span : (c + 1) * span]
    pl.semaphore_wait(barrier, len(partners))
    pre = Gather(pbuf, pzs, pzr, pys, pyr, pcs, pcr)
    for c in range(PCUTS):
        pre.first(c)

    for at in range(1, 4):
        loads[at].wait()
    nkv = new_kv[...].astype(F32)
    new_key = nkv[:, 0, :]
    new_val = nkv[:, 1, :]
    q32[...] = query[...].astype(F32)

    eye = iota((seqs, seqs), 0) == iota((seqs, seqs), 1)

    def column(row):
        return jnp.sum(jnp.where(eye, jnp.broadcast_to(row, (seqs, seqs)), 0.0), axis=1, keepdims=True)

    len_col = column(lens[...].astype(F32))
    live = iota((seqs, CACHE), 1).astype(F32) < len_col
    live = jnp.concatenate([live.astype(F32)] * GROUP, axis=0) > 0.0
    srow = lax.rem(iota((rows, CACHE), 0), seqs)
    loads[4].wait()

    def queries(g):
        return jnp.concatenate(
            [q32[:, (g * GROUP + r) * HEAD : (g * GROUP + r + 1) * HEAD] for r in range(GROUP)], axis=0
        )

    for g in range(KV_HEADS):
        lanes = slice(g * HEAD, (g + 1) * HEAD)
        q = queries(g)
        qb = q.astype(BF16)
        s = jnp.zeros((rows, CACHE), F32)
        for t in range(seqs):
            s = jnp.where(srow == t, mm(qb, cache[t, 0, :, lanes], NT), s)
        s = jnp.where(live, s * factor, NEG)
        nk = jnp.concatenate([new_key[:, lanes]] * GROUP, axis=0)
        own = jnp.sum(q * nk, axis=1, keepdims=True) * factor
        top = jnp.maximum(jnp.max(s, axis=1, keepdims=True), own)
        e = jnp.where(live, jnp.exp(s - top), 0.0)
        e_own = jnp.exp(own - top)
        den = jnp.sum(e, axis=1, keepdims=True) + e_own
        nv = jnp.concatenate([new_val[:, lanes]] * GROUP, axis=0)
        acc = e_own.astype(BF16).astype(F32) * nv
        for t in range(seqs):
            acc = acc + mm(jnp.where(srow == t, e, 0.0).astype(BF16), cache[t, 1, :, lanes])
        acc_ref[g] = acc
        top_ref[g] = jnp.broadcast_to(top, (rows, HEAD))
        den_ref[g] = jnp.broadcast_to(den, (rows, HEAD))
        if g == 5:
            pre.from_z(0)
        if g == 7:
            pre.from_z(1)

    size = CAP * n
    across = CAP * PIECES * n

    def packed_row(x):
        return CAP * PIECES * (lax.rem(x, size) // CAP) + CAP * (x // size) + lax.rem(x, CAP)

    square_at = (across, across)
    perms[0] = (packed_row(iota((across, 1), 0)) == iota(square_at, 1)).astype(F32).astype(BF16)
    perms[1] = (packed_row(iota((1, across), 1)) == iota(square_at, 0)).astype(F32).astype(BF16)

    for at in range(5, 9):
        loads[at].wait()

    count = n * prefix.shape[0]
    square = [jnp.zeros((seqs, HEAD), F32)]

    def attend(c):
        for part in range(KV_HEADS // PCUTS):
            g = c * (KV_HEADS // PCUTS) + part
            lanes = slice(part * HEAD, (part + 1) * HEAD)
            qb = queries(g).astype(BF16)
            keys = pbuf[c, :, 0, :, lanes].reshape(count, HEAD)
            vals = pbuf[c, :, 1, :, lanes].reshape(count, HEAD)
            s = mm(qb, keys, NT) * factor
            best = top_ref[g][:, :1]
            top = jnp.maximum(best, jnp.max(s, axis=1, keepdims=True))
            shrink = jnp.exp(best - top)
            e = jnp.exp(s - top)
            den = den_ref[g][:, :1] * shrink + jnp.sum(e, axis=1, keepdims=True)
            acc = acc_ref[g] * shrink + mm(e.astype(BF16), vals)
            attn = (acc / den).astype(BF16).astype(F32)
            for r in range(GROUP):
                at = slice((g * GROUP + r) * HEAD, (g * GROUP + r + 1) * HEAD)
                h = residual[:, at].astype(F32) + attn[r * seqs : (r + 1) * seqs]
                hidden_ref[:, at] = h
                square[0] = square[0] + h * h

    pre.run(attend, 2)
    square = square[0]

    scale = lax.rsqrt(jnp.sum(square, axis=1, keepdims=True) / d + 1e-5)
    normed = (hidden_ref[...] * scale * gain[...]).astype(BF16)

    routed_row = jnp.zeros((1, seqs), F32)
    for j in range(TOP):
        routed_row = jnp.maximum(routed_row, (ids[j : j + 1, :] == 0).astype(F32))
    routed_col = column(routed_row)
    before = jnp.where(iota((seqs, seqs), 0) < iota((seqs, seqs), 1), routed_col, 0.0)
    rank_row = jnp.sum(before, axis=0, keepdims=True)
    picks = []
    for p in range(PIECES):
        at = (iota((CAP * PIECES, seqs), 0) - CAP * p).astype(F32)
        picks.append(jnp.where((at == rank_row) & (routed_row > 0.0), 1.0, 0.0).astype(BF16))
    tok = Gather(xbuf, xzs, xzr, xys, xyr, xcs, xcr)
    for c in range(CUTS):
        packed = jnp.zeros((CAP * PIECES, thin), F32)
        for p in range(PIECES):
            lo = c * wide + p * thin
            packed = packed + mm(picks[p], normed[:, lo : lo + thin])
        xbuf[c, slot] = packed.astype(BF16)
        tok.first(c)

    logits = mm(normed, router_w[...], NT)
    expo = jnp.exp(logits - jnp.max(logits, axis=1, keepdims=True))
    router = expo / jnp.sum(expo, axis=1, keepdims=True)
    expert = iota((seqs, EXPERTS), 1).astype(F32)
    chosen = jnp.zeros((seqs, EXPERTS), F32)
    for j in range(TOP):
        chosen = chosen + (expert == column(ids[j : j + 1, :].astype(F32))).astype(F32)
    picked = jnp.sum(router * chosen, axis=1, keepdims=True)
    weight = jnp.where(routed_col > 0.0, router[:, :1], 0.0) / picked
    rank_col = column(rank_row)

    loads[9].wait()
    loads[10].wait()

    def gate_up(c):
        stacked = mm(perms[0], xbuf[c].reshape(across, thin)).astype(BF16)
        x = jnp.concatenate([stacked[p * size : (p + 1) * size] for p in range(PIECES)], axis=1)
        gate = mm(x, wg[:, c * wide : (c + 1) * wide], NT)
        upper = mm(x, wu[:, c * wide : (c + 1) * wide], NT)
        if c:
            gate = gate + gate_ref[...]
            upper = upper + upper_ref[...]
        if c < CUTS - 1:
            gate_ref[...] = gate
            upper_ref[...] = upper
        else:
            inner_ref[...] = (gate / (1.0 + jnp.exp(-gate)) * upper).astype(BF16)

    tok.run(gate_up)

    loads[11].wait()

    def hop1(c):
        src = msg.at[c, pl.ds((1 - core) * half, half)]
        return remote(src, got_core.at[c], csend.at[c], crecv.at[c], core_peer)

    def hop2(c):
        src = sum_core.at[c, pl.ds((1 - yy) * hi_n, hi_n)]
        return remote(src, got_y.at[c], ysend.at[c], yrecv.at[c], y_peer)

    def hop3(c, k):
        h = lax.rem(hi + k, hi_n)
        return remote(
            sum_y.at[c, h], got_z.at[c, k - 1], zsend.at[c, k - 1], zrecv.at[c, k - 1], z_peer(k)
        )

    def work(c):
        y = mm(inner_ref[...], wd[:, c * wide : (c + 1) * wide]).astype(BF16)
        for piece in range(PIECES):
            ystack[c, piece * size : (piece + 1) * size, :] = y[:, piece * thin : (piece + 1) * thin]
        full = mm(perms[1], ystack[c]).astype(BF16)
        msg[c] = full.reshape(n, CAP * PIECES, thin)
        hop1(c).start()

    def add_core(c):
        hop1(c).wait_recv()
        total = msg[c, pl.ds(core * half, half)].astype(F32) + got_core[c].astype(F32)
        sum_core[c] = total.astype(BF16)
        hop2(c).start()

    def add_y(c):
        hop2(c).wait_recv()
        total = sum_core[c, pl.ds(yy * hi_n, hi_n)].astype(F32) + got_y[c].astype(F32)
        sum_y[c] = total.astype(BF16)
        for k in range(1, hi_n):
            hop3(c, k).start()

    def finish(c):
        total = sum_y[c, hi].astype(F32)
        for k in range(1, hi_n):
            hop3(c, k).wait_recv()
            total = total + got_z[c, k - 1].astype(F32)
        for piece in range(PIECES):
            lo = c * wide + piece * thin
            y = jnp.zeros((seqs, thin), F32)
            for k in range(CAP):
                mine = (rank_col == float(k)) & (routed_col > 0.0)
                at = piece * CAP + k
                y = y + jnp.where(mine, total[at : at + 1, :], 0.0)
            out[:, lo : lo + thin] = (hidden_ref[:, lo : lo + thin] + weight * y).astype(BF16)

    work(0)
    work(1)
    for c in range(2, CUTS):
        work(c)
        add_core(c - 2)
    add_core(CUTS - 2)
    add_core(CUTS - 1)
    for c in range(CUTS):
        add_y(c)
    for c in range(CUTS):
        finish(c)

    pre.drain()
    tok.drain()
    for c in range(CUTS):
        hop1(c).wait_send()
        hop2(c).wait_send()
        for k in range(1, hi_n):
            hop3(c, k).wait_send()


def body(n, query, new_kv, cache_kv, cache_len, prefix_kv, residual_in, norm_gain, router_w, expert_ids, w_gate, w_up, w_down):
    seqs, d = query.shape
    ff = w_down.shape[0]
    per = prefix_kv.shape[0]
    width = KV_HEADS * HEAD
    rows = seqs * GROUP
    wide = d // CUTS
    thin = wide // PIECES
    packs = CAP * PIECES
    hi_n = n // 4
    hops = max(hi_n - 1, 1)
    vmem = pl.BlockSpec(memory_space=pltpu.VMEM)
    hbm = pl.BlockSpec(memory_space=pl.ANY)
    dma = pltpu.SemaphoreType.DMA
    return pl.pallas_call(
        functools.partial(kernel, n),
        out_shape=jax.ShapeDtypeStruct((seqs, d), BF16),
        in_specs=[hbm] * 12,
        out_specs=vmem,
        scratch_shapes=[
            pltpu.VMEM((seqs, d), BF16),
            pltpu.VMEM((seqs, 2, width), BF16),
            pltpu.VMEM((seqs, 2, CACHE, width), BF16),
            pltpu.VMEM((1, seqs), jnp.int32),
            pltpu.VMEM((per, 2, width), BF16),
            pltpu.VMEM((seqs, d), BF16),
            pltpu.VMEM((1, d), F32),
            pltpu.VMEM((EXPERTS, d), BF16),
            pltpu.VMEM((TOP, seqs), jnp.int32),
            pltpu.VMEM((ff, d), BF16),
            pltpu.VMEM((ff, d), BF16),
            pltpu.VMEM((ff, d), BF16),
            pltpu.VMEM((PCUTS, n, 2, per, width // PCUTS), BF16),
            pltpu.VMEM((seqs, d), F32),
            pltpu.VMEM((KV_HEADS, rows, HEAD), F32),
            pltpu.VMEM((KV_HEADS, rows, HEAD), F32),
            pltpu.VMEM((KV_HEADS, rows, HEAD), F32),
            pltpu.VMEM((seqs, d), F32),
            pltpu.VMEM((CUTS, n, packs, thin), BF16),
            pltpu.VMEM((2, n * packs, n * packs), BF16),
            pltpu.VMEM((CAP * n, ff), F32),
            pltpu.VMEM((CAP * n, ff), F32),
            pltpu.VMEM((CAP * n, ff), BF16),
            pltpu.VMEM((CUTS, n * packs, thin), BF16),
            pltpu.VMEM((CUTS, n, packs, thin), BF16),
            pltpu.VMEM((CUTS, n // 2, packs, thin), BF16),
            pltpu.VMEM((CUTS, n // 2, packs, thin), BF16),
            pltpu.VMEM((CUTS, hi_n, packs, thin), BF16),
            pltpu.VMEM((CUTS, hi_n, packs, thin), BF16),
            pltpu.VMEM((CUTS, hops, packs, thin), BF16),
            dma((12,)),
            dma((PCUTS, hops)),
            dma((PCUTS, hops)),
            dma((PCUTS,)),
            dma((PCUTS,)),
            dma((PCUTS, 2)),
            dma((PCUTS, 2)),
            dma((CUTS, hops)),
            dma((CUTS, hops)),
            dma((CUTS,)),
            dma((CUTS,)),
            dma((CUTS, 2)),
            dma((CUTS, 2)),
            dma((CUTS,)),
            dma((CUTS,)),
            dma((CUTS,)),
            dma((CUTS,)),
            dma((CUTS, hops)),
            dma((CUTS, hops)),
        ],
        compiler_params=pltpu.CompilerParams(
            collective_id=0, has_side_effects=True, vmem_limit_bytes=60 * 1024 * 1024
        ),
        cost_estimate=pl.CostEstimate(
            flops=6 * CAP * n * d * ff, bytes_accessed=6 * d * ff + 2 * cache_kv.size, transcendentals=0
        ),
    )(
        query,
        new_kv,
        cache_kv,
        cache_len.reshape(1, seqs),
        prefix_kv,
        residual_in,
        norm_gain.reshape(1, d),
        router_w.T,
        expert_ids.T,
        w_gate.T,
        w_up.T,
        w_down,
    )


def solution(mesh):
    return jax.shard_map(
        functools.partial(body, mesh.shape["node"]),
        mesh=mesh,
        in_specs=(
            P(("groups", "node"), None),
            P(("groups", "node"), None, None),
            P(("groups", "node"), None, None, None),
            P(("groups", "node")),
            P(("groups", "node"), None, None),
            P(("groups", "node"), None),
            P(),
            P(),
            P(("groups", "node"), None),
            P(None, "node"),
            P(None, "node"),
            P("node", None),
        ),
        out_specs=P(("groups", "node"), None),
        check_vma=False,
    )
```
